32 devices in a mesh: path: 4 (over x, core), shard: 8 (over z, y).
Axes of the slice: x: 2, y: 2, z: 4, core: 2. Of those that a mesh axis runs over, the one named last changes fastest.
Arguments:
- tokens: bfloat16 [384, 2048], P(('path', 'shard')), may hold values from -6 to 6
- routes: int32 [384, 1], P(('path', 'shard')), may hold values from 0 to 3; in each aligned block of 12 rows (0 to 11, 12 to 23, ...) at most 4 rows name the same one
- cotangent: bfloat16 [384, 2048], P(('path', 'shard')), may hold values from -6 to 6
- gains: bfloat16 [4, 2, 2048], P('path'), may hold values from 0.099609375 to 1.8984375
- w_in: bfloat16 [4, 2, 2048, 8192], P('path', None, None, 'shard'), may hold values from -0.125 to 0.125
- w_out: bfloat16 [4, 2, 8192, 2048], P('path', None, 'shard'), may hold values from -0.0625 to 0.0625
- partners: int32 [2, 4], replicated, may hold values from 0 to 3, as said below
Outputs:
- delta_in: bfloat16 [4, 2, 2048, 8192], P('path', None, None, 'shard')
- delta_out: bfloat16 [4, 2, 8192, 2048], P('path', None, 'shard')
The draws below stay inside these ranges and needn't reach their ends.
Inputs may be any that keep to these rules, and one draw needn't show every extreme that they name: `routes`: in each device's block of 12 rows at most 4 rows name one path, and some path gets exactly 4 rows of some block. Each row pairs the paths: partners[l, partners[l, p]] = p and partners[l, p] != p.
All inputs are finite; a program needn't handle non-finite values.
Results may differ from the reference program's by a relative error of at most 0.03.
Values may be sent and summed in bfloat16 or wider, within the bound.
No kernel may reach another device: no remote copies, remote signals or barrier semaphores. Data moves between devices by JAX's collectives and lax.ppermute only.
A program may use at most 128 MiB of HBM per device.

```python
import math
import jax
import jax.numpy as jnp
import numpy as np
from jax import lax

D = 2048
FF = 8192
SLOTS = 16
LEVELS = 2
TOK_DEV = 12
CAP = 4
PATH_ROWS = 128
TOKENS = 384
N_PATH = 4
N_SHARD = 8


def draw_partners(key, part):
    rows = []
    for level in range(LEVELS):
        order = jax.random.permutation(jax.random.fold_in(key, 17 + level), N_PATH).astype(jnp.int32)
        pairs = order.reshape(N_PATH // 2, 2)
        mate = jnp.zeros((N_PATH,), jnp.int32)
        mate = mate.at[pairs[:, 0]].set(pairs[:, 1])
        mate = mate.at[pairs[:, 1]].set(pairs[:, 0])
        rows.append(mate)
    return jnp.stack(rows)


def levels(stream_key, shape, shards, least, largest):
    factor_of, own = 1.0, jax.random.fold_in(stream_key, 6)
    for position, blocks in shards:
        draws = jnp.exp(jax.random.uniform(jax.random.fold_in(own, position), (blocks,), jnp.float32, least / len(shards), largest / len(shards)))
        factor_of = factor_of * jnp.repeat(draws, shape[position] // blocks).reshape([-1 if axis == position else 1 for axis in range(len(shape))])
    return factor_of


def deal_out(key, own, number, rows, count, top, reach, lean):
    ranking = jax.random.permutation(key, count)
    heavy_load, usual = shares(count, rows * top, reach, lean, True), shares(count, rows * top, reach, lean, False)
    places = jnp.arange(count)

    def named(sizes, offset_by):
        used = int((sizes > 0).sum())
        fixed = max(1, used // 4)
        shifted = fixed + (places - fixed + offset_by * (used - fixed)) % max(1, count - fixed)
        return jnp.zeros((count,), jnp.int32).at[ranking[jnp.where(places < fixed, places, shifted)]].set(jnp.asarray(sizes, jnp.int32))

    sizes = jnp.where(number % 4 == 0, named(heavy_load, number // 4), named(usual, number - number // 4 - 1))
    mixed = jax.random.permutation(jax.random.fold_in(own, 3), count)
    donor, taker = mixed[0:count // 2 * 2:2], mixed[1:count // 2 * 2:2]
    room = jnp.minimum(sizes[donor] - 1, reach - sizes[taker]) // 2
    room = jnp.where((donor == ranking[0]) | (taker == ranking[0]) | (sizes[taker] == 0), 0, jnp.maximum(room, 0))
    shifted = jax.random.randint(jax.random.fold_in(own, 4), (count // 2,), 0, 1 << 20) % (room + 1)
    sizes = sizes.at[donor].add(-shifted).at[taker].add(shifted)
    items = jnp.searchsorted(jnp.cumsum(sizes), jnp.arange(rows * top), side="right").astype(jnp.int32)
    grid = items.reshape(top, rows).T
    grid = grid[jax.random.permutation(jax.random.fold_in(own, 1), rows)]
    offset_by = jax.random.randint(jax.random.fold_in(own, 2), (rows, 1), 0, top)
    return jnp.take_along_axis(grid, (jnp.arange(top)[None, :] + offset_by) % top, axis=1)


def shares(amount, total, limit, skew, full):
    weights = [(1 << 20) // math.isqrt(standing ** skew) + 1 for standing in range(1, amount + 1)]
    largest = limit if full else min(limit, max(-(-total // amount), total * weights[0] // sum(weights)))
    least = 1 if total - largest >= amount - 1 else 0
    holding, rest = [largest] + [least] * (amount - 1), total - largest - least * (amount - 1)
    while rest > 0:
        movable = [i for i in range(1, amount) if holding[i] < largest] or [i for i in range(1, amount) if holding[i] < limit]
        mass, budget = sum([weights[i] for i in movable]), rest
        for i in movable:
            more = min(limit - holding[i], max(1, budget * weights[i] // mass), rest)
            holding[i] = holding[i] + more
            rest = rest - more
    return np.array(holding)


def normal_values(stream_key, dims, width, limit, shards=(), held_as=jnp.bfloat16):
    drawn = width * jax.random.normal(stream_key, dims, jnp.float32)
    if shards:
        drawn = drawn * levels(stream_key, dims, shards, -0.22, 0.18)
    return jnp.clip(drawn, -limit, limit).astype(held_as)


def setup_inputs(seed: int = 0) -> dict:
    streams_of = jax.random.split(jax.random.key(seed), 8)
    tokens = normal_values(streams_of[0], (TOKENS, D), 1.0, 6.0, ((0, 32),))
    routes_keys = jax.random.split(jax.random.fold_in(streams_of[1], 1), TOKENS // TOK_DEV)
    routes_turns = jax.random.permutation(jax.random.fold_in(streams_of[1], 3), TOKENS // TOK_DEV)
    routes = jax.vmap(lambda own, number: deal_out(jax.random.fold_in(streams_of[1], 2), own, number, TOK_DEV, N_PATH, 1, CAP, 2))(routes_keys, routes_turns).reshape((TOKENS, 1))
    cotangent = normal_values(streams_of[2], (TOKENS, D), 1.0, 6.0, ((0, 32),))
    gains = jnp.clip(1.0 + 0.18 * jax.random.normal(streams_of[3], (N_PATH, LEVELS, D), jnp.float32), 0.099609375, 1.8984375).astype(jnp.bfloat16)
    w_in = normal_values(streams_of[4], (N_PATH, LEVELS, D, FF), D ** -0.5, 0.125, ((0, 4), (3, 8)))
    w_out = normal_values(streams_of[5], (N_PATH, LEVELS, FF, D), FF ** -0.5, 0.0625, ((0, 4), (2, 8)))
    partners = draw_partners(jax.random.fold_in(streams_of[7], 71), 0)
    return {"tokens": tokens, "routes": routes, "cotangent": cotangent, "gains": gains, "w_in": w_in, "w_out": w_out, "partners": partners}


def norm_value(v, gain):
    return v * lax.rsqrt(lax.optimization_barrier(jnp.mean(v * v, axis=-1, keepdims=True)) + 1e-05) * gain.astype(jnp.float32)

def norm_pull(h, gain, grad):

    def value(v):
        return norm_value(v, gain)
    return jax.vjp(value, h.astype(jnp.float32))[1](grad)[0]

def gelu_pull(pre, grad):
    return jax.vjp(jax.nn.gelu, pre)[1](grad)[0]

def grouped(left, right_t):
    rows = left.shape[0]
    left3 = left.astype(jnp.float32).reshape(rows, N_SHARD, -1)
    right3 = right_t.astype(jnp.float32).reshape(N_SHARD, left3.shape[2], -1)
    parts = jnp.einsum('rsf,sfd->srd', left3, right3).astype(jnp.bfloat16)
    return lax.optimization_barrier(jnp.sum(parts.astype(jnp.float32), axis=0))

def one_path(inputs):
    x, dy, gain, wi, wo = inputs
    n1 = norm_value(x.astype(jnp.float32), gain[0]).astype(jnp.bfloat16)
    a1 = jnp.dot(n1, wi[0], preferred_element_type=jnp.float32)
    u1 = jax.nn.gelu(a1).astype(jnp.bfloat16)
    y1 = grouped(u1, wo[0])
    h1 = (x.astype(jnp.float32) + y1).astype(jnp.bfloat16)
    n2 = norm_value(h1.astype(jnp.float32), gain[1]).astype(jnp.bfloat16)
    a2 = jnp.dot(n2, wi[1], preferred_element_type=jnp.float32)
    u2 = jax.nn.gelu(a2).astype(jnp.bfloat16)
    g_out2 = jnp.dot(u2.T, dy, preferred_element_type=jnp.float32)
    du2 = jnp.dot(dy, wo[1].T, preferred_element_type=jnp.float32)
    da2 = gelu_pull(a2, du2).astype(jnp.bfloat16)
    g_in2 = jnp.dot(n2.T, da2, preferred_element_type=jnp.float32)
    dn2 = grouped(da2, wi[1].T)
    dh1 = (dy.astype(jnp.float32) + norm_pull(h1, gain[1], dn2)).astype(jnp.bfloat16)
    g_out1 = jnp.dot(u1.T, dh1, preferred_element_type=jnp.float32)
    du1 = jnp.dot(dh1, wo[0].T, preferred_element_type=jnp.float32)
    da1 = gelu_pull(a1, du1).astype(jnp.bfloat16)
    g_in1 = jnp.dot(n1.T, da1, preferred_element_type=jnp.float32)
    return (jnp.stack([g_in1, g_in2]), jnp.stack([g_out1, g_out2]))

def reference(tokens, routes, cotangent, gains, w_in, w_out, partners):
    route = routes[:, 0].reshape(N_PATH, N_SHARD, TOK_DEV)
    order = jnp.arange(TOK_DEV, dtype=jnp.int32)
    same = (route[..., :, None] == route[..., None, :]) & (order[None, :] < order[:, None])
    rank = lax.optimization_barrier(jnp.sum(same.astype(jnp.int32), axis=-1))
    shard_ix = jnp.arange(N_SHARD, dtype=jnp.int32)[None, :, None]
    source = jnp.arange(N_PATH, dtype=jnp.int32)[:, None, None]
    place = (route * PATH_ROWS + shard_ix * SLOTS + source * CAP + rank).reshape(-1).astype(jnp.int32)
    x = jnp.zeros((N_PATH * PATH_ROWS, D), jnp.bfloat16).at[place].set(tokens).reshape(N_PATH, PATH_ROWS, D)
    dy = jnp.zeros((N_PATH * PATH_ROWS, D), jnp.bfloat16).at[place].set(cotangent).reshape(N_PATH, PATH_ROWS, D)
    g_in, g_out = lax.map(one_path, (x, dy, gains, w_in, w_out))
    scale = 1.0 / jnp.sqrt(jnp.float32(PATH_ROWS))
    e_in = (-g_in * scale).astype(jnp.bfloat16)
    e_out = (-g_out * scale).astype(jnp.bfloat16)
    outs_in = []
    outs_out = []
    for level in range(LEVELS):
        mate = partners[level]
        own_in = e_in[:, level].astype(jnp.float32)
        own_out = e_out[:, level].astype(jnp.float32)
        outs_in.append(((own_in + own_in[mate]) * 0.5).astype(jnp.bfloat16))
        outs_out.append(((own_out + own_out[mate]) * 0.5).astype(jnp.bfloat16))
    return (jnp.stack(outs_in, axis=1), jnp.stack(outs_out, axis=1))
```

```python
import functools

import jax
import jax.numpy as jnp
from jax import lax
from jax.experimental import pallas as pl
from jax.experimental.pallas import tpu as pltpu
from jax.sharding import PartitionSpec as P

SLOTS = 16


def norm_value(v, gain):
    return v * lax.rsqrt(jnp.mean(v * v, axis=-1, keepdims=True) + 1e-05) * gain.astype(jnp.float32)


def norm_pull(h, gain, grad):

    def value(v):
        return norm_value(v, gain)

    return jax.vjp(value, h.astype(jnp.float32))[1](grad)[0]


def gelu_pull(pre, grad):
    return jax.vjp(jax.nn.gelu, pre)[1](grad)[0]


def gather_shard(own):
    shards = lax.axis_size("shard")
    spread = jnp.broadcast_to(own[None], (shards, *own.shape))
    got = lax.all_to_all(spread, "shard", split_axis=0, concat_axis=0, tiled=True)
    return got.reshape(shards * own.shape[0], own.shape[1])


def reduce_shard(part):
    shards = lax.axis_size("shard")
    blocks = part.reshape(shards, part.shape[0] // shards, part.shape[1])
    got = lax.all_to_all(blocks, "shard", split_axis=0, concat_axis=0, tiled=True)
    return jnp.sum(got.astype(jnp.float32), axis=0)


def from_mate(value, mate):
    paths = lax.axis_size("path")
    if paths == 4:
        near = lax.ppermute(value, "path", [(i, i ^ 1) for i in range(4)])
        sent = jnp.where(mate == 3, near, value)
        far = lax.ppermute(sent, "path", [(i, i ^ 2) for i in range(4)])
        return near, far
    me = lax.axis_index("path")
    behind = (me - (me ^ mate)) % paths
    mine = value
    for shift in range(1, paths):
        got = lax.ppermute(value, "path", [(i, (i + shift) % paths) for i in range(paths)])
        mine = jnp.where(behind == shift, got, mine)
    return mine, mine


def pair_grad_kernel(factor, mate_ref, a_ref, an_ref, af_ref, b_ref, bn_ref, bf_ref, *rest):
    out_ref = rest[-1]
    near = mate_ref[0] == 1
    contract = (((0,), (0,)), ((), ()))
    own = lax.dot_general(a_ref[...], b_ref[...], contract, preferred_element_type=jnp.float32)
    a_mate = jnp.where(near, an_ref[...], af_ref[...])
    b_mate = jnp.where(near, bn_ref[...], bf_ref[...])
    other = lax.dot_general(a_mate, b_mate, contract, preferred_element_type=jnp.float32)
    out_ref[0, 0] = ((own + other) * factor).astype(jnp.bfloat16)


def pair_grad(mate, a, a_mate, b, b_mate, level, before):
    rows, left = a.shape
    right = b.shape[1]
    factor = -0.5 / rows**0.5
    block = min(256, left)
    a_spec = pl.BlockSpec((rows, block), lambda i: (0, i))
    b_spec = pl.BlockSpec((rows, right), lambda i: (0, 0))
    operands = [mate.reshape(1), a, *a_mate, b, *b_mate]
    in_specs = [pl.BlockSpec(memory_space=pltpu.SMEM), a_spec, a_spec, a_spec, b_spec, b_spec, b_spec]
    aliases = {}
    if before is not None:
        aliases = {len(operands): 0}
        operands.append(before)
        in_specs.append(pl.BlockSpec(memory_space=pl.ANY))
    return pl.pallas_call(
        functools.partial(pair_grad_kernel, factor),
        grid=(left // block,),
        in_specs=in_specs,
        out_specs=pl.BlockSpec((1, 1, block, right), lambda i: (0, level, i, 0)),
        out_shape=jax.ShapeDtypeStruct((1, 2, left, right), jnp.bfloat16),
        input_output_aliases=aliases,
        compiler_params=pltpu.CompilerParams(vmem_limit_bytes=32 * 1024 * 1024),
        cost_estimate=pl.CostEstimate(
            flops=4 * rows * left * right, bytes_accessed=2 * left * right + 6 * rows * (left + right), transcendentals=0
        ),
    )(*operands)


def body(tokens, routes, cotangent, gains, w_in, w_out, partners):
    paths = lax.axis_size("path")
    shards = lax.axis_size("shard")
    slots = SLOTS
    cap = slots // paths
    width = tokens.shape[1]
    me = lax.axis_index("path")
    mate_low = partners[0, me] ^ me
    mate_high = partners[1, me] ^ me
    route = routes[:, 0]
    order = jnp.arange(route.shape[0], dtype=jnp.int32)
    same = (route[:, None] == route[None, :]) & (order[None, :] < order[:, None])
    rank = jnp.sum(same.astype(jnp.int32), axis=1)
    target = route * cap + rank
    select = (jnp.arange(slots, dtype=jnp.int32)[:, None] == target[None, :]).astype(jnp.bfloat16)
    packed_x = jnp.dot(select, tokens, preferred_element_type=jnp.float32).astype(jnp.bfloat16)
    packed_dy = jnp.dot(select, cotangent, preferred_element_type=jnp.float32).astype(jnp.bfloat16)

    spread = jnp.broadcast_to(packed_x.reshape(paths, 1, cap, width), (paths, shards, cap, width))
    got = lax.all_to_all(
        spread.reshape(paths * shards, cap, width), ("path", "shard"), split_axis=0, concat_axis=0, tiled=True
    ).reshape(paths, shards, cap, width)
    full_x = got.transpose(1, 0, 2, 3).reshape(shards * slots, width)
    own_x = lax.dynamic_slice_in_dim(full_x, lax.axis_index("shard") * slots, slots, 0)

    got_dy = lax.all_to_all(packed_dy.reshape(paths, cap, width), "path", split_axis=0, concat_axis=0, tiled=True)
    own_dy = got_dy.reshape(slots, width)
    full_dy = gather_shard(own_dy)

    gain_low = gains[0, 0]
    gain_high = gains[0, 1]
    wi_low = w_in[0, 0]
    wi_high = w_in[0, 1]
    wo_low = w_out[0, 0]
    wo_high = w_out[0, 1]
    n1 = norm_value(full_x.astype(jnp.float32), gain_low).astype(jnp.bfloat16)
    a1 = jnp.dot(n1, wi_low, preferred_element_type=jnp.float32)
    u1 = jax.nn.gelu(a1).astype(jnp.bfloat16)
    part_low = jnp.dot(u1, wo_low, preferred_element_type=jnp.float32).astype(jnp.bfloat16)
    n1_mate = from_mate(n1, mate_low)
    u1_mate = from_mate(u1, mate_low)
    mixed_own = reduce_shard(part_low)
    h_own = (own_x.astype(jnp.float32) + mixed_own).astype(jnp.bfloat16)
    full_h = gather_shard(h_own)

    du2 = jnp.dot(full_dy, wo_high.T, preferred_element_type=jnp.float32)
    dy_mate = from_mate(full_dy, mate_high)
    n2 = norm_value(full_h.astype(jnp.float32), gain_high).astype(jnp.bfloat16)
    a2 = jnp.dot(n2, wi_high, preferred_element_type=jnp.float32)
    u2 = jax.nn.gelu(a2).astype(jnp.bfloat16)
    da2 = gelu_pull(a2, du2).astype(jnp.bfloat16)
    part_back = jnp.dot(da2, wi_high.T, preferred_element_type=jnp.float32).astype(jnp.bfloat16)
    u2_mate = from_mate(u2, mate_high)
    n2_mate = from_mate(n2, mate_high)
    da2_mate = from_mate(da2, mate_high)
    back_own = reduce_shard(part_back)
    dh_own = (own_dy.astype(jnp.float32) + norm_pull(h_own, gain_high, back_own)).astype(jnp.bfloat16)
    full_dh = gather_shard(dh_own)

    delta_in = pair_grad(mate_high, n2, n2_mate, da2, da2_mate, 1, None)
    delta_out = pair_grad(mate_high, u2, u2_mate, full_dy, dy_mate, 1, None)

    du1 = jnp.dot(full_dh, wo_low.T, preferred_element_type=jnp.float32)
    da1 = gelu_pull(a1, du1).astype(jnp.bfloat16)
    dh_mate = from_mate(full_dh, mate_low)
    da1_mate = from_mate(da1, mate_low)
    delta_out = pair_grad(mate_low, u1, u1_mate, full_dh, dh_mate, 0, delta_out)
    delta_in = pair_grad(mate_low, n1, n1_mate, da1, da1_mate, 0, delta_in)
    return (delta_in, delta_out)


def solution(mesh):
    in_specs = (
        P(("path", "shard"), None),
        P(("path", "shard"), None),
        P(("path", "shard"), None),
        P("path", None, None),
        P("path", None, None, "shard"),
        P("path", None, "shard", None),
        P(),
    )
    out_specs = (P("path", None, None, "shard"), P("path", None, "shard", None))
    return jax.shard_map(body, mesh=mesh, in_specs=in_specs, out_specs=out_specs, check_vma=False)
```

```python
import functools

import jax
import jax.numpy as jnp
from jax import lax
from jax.experimental import pallas as pl
from jax.experimental.pallas import tpu as pltpu
from jax.sharding import PartitionSpec as P

SLOTS = 16
BLOCK = 256
ROOT = 0.7978845608028654
CUBE = 0.044715
NT = (((1,), (1,)), ((), ()))
TN = (((0,), (0,)), ((), ()))
PARAMS = pltpu.CompilerParams(vmem_limit_bytes=16 * 1024 * 1024)
SMALL = pltpu.CompilerParams(vmem_limit_bytes=56 * 1024 * 1024)
IN_VMEM = pl.BlockSpec(memory_space=pltpu.VMEM)
IN_SMEM = pl.BlockSpec(memory_space=pltpu.SMEM)
ANYWHERE = pl.BlockSpec(memory_space=pl.ANY)
FREE = pl.CostEstimate(flops=0, bytes_accessed=0, transcendentals=0)


def bf16(*shape):
    return jax.ShapeDtypeStruct(shape, jnp.bfloat16)


def f32(*shape):
    return jax.ShapeDtypeStruct(shape, jnp.float32)


def cuts(size, step=BLOCK):
    step = min(step, size)
    return [pl.ds(start, step) for start in range(0, size, step)]


def tie(*values):
    return lax.optimization_barrier(values)


def call(kernel, name, where, arrays, outs):
    operands = [] if where is None else [where]
    return pl.pallas_call(
        kernel,
        in_specs=[IN_SMEM] * len(operands) + [IN_VMEM] * len(arrays),
        out_specs=[IN_VMEM] * len(outs),
        out_shape=outs,
        compiler_params=PARAMS,
        cost_estimate=FREE,
        name=name,
    )(*operands, *arrays)


def norm_value(v, gain):
    return v * lax.rsqrt(jnp.mean(v * v, axis=-1, keepdims=True) + 1e-05) * gain.astype(jnp.float32)


def gelu_both(a):
    t = jnp.tanh(ROOT * (a + CUBE * (a * a * a)))
    half = 0.5 * (1.0 + t)
    slope = half + 0.5 * a * (1.0 - t * t) * (ROOT * (1.0 + (3.0 * CUBE) * (a * a)))
    return a * half, slope


def slots_of_rows(routes_ref, cap, flip):
    count = routes_ref.shape[0]
    down = lax.broadcasted_iota(jnp.int32, (count, count), 0)
    along = lax.broadcasted_iota(jnp.int32, (count, count), 1)
    route_down = jnp.zeros((count, count), jnp.int32)
    route_along = jnp.zeros((count, count), jnp.int32)
    for r in range(count):
        route = routes_ref[r]
        route_down = jnp.where(down == r, route, route_down)
        route_along = jnp.where(along == r, route, route_along)
    earlier = jnp.where((route_down == route_along) & (down < along), 1, 0)
    rank = jnp.sum(earlier, axis=0, keepdims=True)
    return (route_along[0:1, :] ^ flip) * cap + rank


def pack_kernel(copies, flip_ref, routes_ref, rows_ref, *out_refs):
    count = routes_ref.shape[0]
    cap = out_refs[0].shape[-2]
    slots = slots_of_rows(routes_ref, cap, flip_ref[0])
    for group in range(SLOTS // cap):
        want = group * cap + lax.broadcasted_iota(jnp.int32, (cap, count), 0)
        pick = (want == slots).astype(jnp.float32).astype(jnp.bfloat16)
        value = jnp.dot(pick, rows_ref[...], preferred_element_type=jnp.float32).astype(jnp.bfloat16)
        if copies == 0:
            out_refs[group][...] = value
        for copy in range(copies):
            out_refs[0][group * copies + copy] = value


def pack(flip, routes, rows, paths, copies):
    cap, width = SLOTS // paths, rows.shape[1]
    outs = [bf16(paths * copies, cap, width)] if copies else [bf16(cap, width)] * paths
    got = pl.pallas_call(
        functools.partial(pack_kernel, copies),
        in_specs=[IN_SMEM, IN_SMEM, IN_VMEM],
        out_specs=[IN_VMEM] * len(outs),
        out_shape=outs,
        compiler_params=SMALL,
        cost_estimate=FREE,
        name="pack",
    )(flip.reshape(1), routes, rows)
    return got[0] if copies else got


def settle_kernel(where_ref, got_ref, x_ref, own_ref, spread_ref):
    count, rows, _ = got_ref.shape
    total = x_ref[pl.ds(pl.multiple_of(where_ref[2] * rows, rows), rows), :].astype(jnp.float32)
    for i in range(count):
        total += got_ref[i].astype(jnp.float32)
    total = total.astype(jnp.bfloat16)
    own_ref[...] = total
    for i in range(count):
        spread_ref[i] = total


def settle(where, got, x):
    count, rows, width = got.shape
    return call(settle_kernel, "settle", where, [got, x], [bf16(rows, width), bf16(count, rows, width)])


def settle_back_kernel(where_ref, got_ref, dy_ref, h_ref, gain_ref, own_ref, spread_ref):
    count, rows, _ = got_ref.shape
    grad = got_ref[0].astype(jnp.float32)
    for i in range(1, count):
        grad += got_ref[i].astype(jnp.float32)
    grad = grad * gain_ref[1:2, :].astype(jnp.float32)
    h = h_ref[...].astype(jnp.float32)
    scale = lax.rsqrt(jnp.mean(h * h, axis=-1, keepdims=True) + 1e-05)
    unit = h * scale
    pull = scale * (grad - unit * jnp.mean(grad * unit, axis=-1, keepdims=True))
    dy = dy_ref[pl.ds(pl.multiple_of(where_ref[2] * rows, rows), rows), :].astype(jnp.float32)
    total = (dy + pull).astype(jnp.bfloat16)
    own_ref[...] = total
    for i in range(count):
        spread_ref[i] = total


def settle_back(where, got, dy, h_own, gains):
    count, rows, width = got.shape
    outs = [bf16(rows, width), bf16(count, rows, width)]
    return call(settle_back_kernel, "settle_back", where, [got, dy, h_own, gains], outs)


def low_kernel(x_ref, gain_ref, wi_ref, wo_ref, n_ref, u_ref, slope_ref, part_ref):
    n_ref[...] = norm_value(x_ref[...].astype(jnp.float32), gain_ref[0:1, :]).astype(jnp.bfloat16)
    for cut in cuts(wi_ref.shape[1]):
        a = jnp.dot(n_ref[...], wi_ref[:, cut], preferred_element_type=jnp.float32)
        u, slope = gelu_both(a)
        u_ref[:, cut] = u.astype(jnp.bfloat16)
        slope_ref[:, cut] = slope
    for cut in cuts(wo_ref.shape[1]):
        part = jnp.dot(u_ref[...], wo_ref[:, cut], preferred_element_type=jnp.float32)
        part_ref[:, cut] = part.astype(jnp.bfloat16)


def low_forward(x, gains, wi, wo):
    rows, width = x.shape
    hidden = wi.shape[-1]
    outs = [bf16(rows, width), bf16(rows, hidden), f32(rows, hidden), bf16(rows, width)]
    return call(low_kernel, "low_forward", None, [x, gains, wi, wo], outs)


def high_kernel(h_ref, gain_ref, wi_ref, du_ref, n_ref, pair_ref, part_ref):
    hidden = wi_ref.shape[1]
    n_ref[...] = norm_value(h_ref[...].astype(jnp.float32), gain_ref[1:2, :]).astype(jnp.bfloat16)
    for cut in cuts(hidden):
        a = jnp.dot(n_ref[...], wi_ref[:, cut], preferred_element_type=jnp.float32)
        u, slope = gelu_both(a)
        pair_ref[:, cut] = u.astype(jnp.bfloat16)
        pair_ref[:, pl.ds(hidden + cut.start, cut.size)] = (slope * du_ref[:, cut]).astype(jnp.bfloat16)
    for cut in cuts(wi_ref.shape[0]):
        part = lax.dot_general(pair_ref[:, hidden:], wi_ref[cut, :], NT, preferred_element_type=jnp.float32)
        part_ref[:, cut] = part.astype(jnp.bfloat16)


def high_both(h, gains, wi, du):
    rows, width = h.shape
    outs = [bf16(rows, width), bf16(rows, 2 * wi.shape[-1]), bf16(rows, width)]
    return call(high_kernel, "high_both", None, [h, gains, wi, du], outs)


def places(order, rows, path, shard):
    to = lax.broadcasted_iota(jnp.int32, (rows, rows), 0)
    source = lax.broadcasted_iota(jnp.int32, (rows, rows), 1)
    if order == "dispatch":
        far = ((to >> 2) & 7) ^ shard
        block = ((far & 1) << 2) | (far & 2) | (far >> 2)
        wanted = block * 16 + ((to >> 5) ^ path) * 4 + (to & 3)
    else:
        far = (to >> 4) ^ shard
        block = ((far & 1) << 2) | (far & 2) | (far >> 2)
        wanted = block * 16 + (to & 15)
    return (source == wanted).astype(jnp.float32).astype(jnp.bfloat16)


def high_grad_kernel(ordered, where_ref, raw_ref, wo_ref, dy_ref, du_ref):
    if ordered:
        dy_ref[...] = raw_ref[...]
    else:
        pick = places("dispatch", raw_ref.shape[0], where_ref[3], where_ref[2])
        dy_ref[...] = jnp.dot(pick, raw_ref[...], preferred_element_type=jnp.float32).astype(jnp.bfloat16)
    for cut in cuts(wo_ref.shape[0]):
        du_ref[:, cut] = lax.dot_general(dy_ref[...], wo_ref[cut, :], NT, preferred_element_type=jnp.float32)


def high_grad(where, raw, wo, ordered):
    rows, width = raw.shape
    kernel = functools.partial(high_grad_kernel, ordered)
    return call(kernel, "high_grad", where, [raw, wo], [bf16(rows, width), f32(rows, wo.shape[-2])])


def low_grad_kernel(dh_ref, wo_ref, slope_ref, da_ref):
    for cut in cuts(wo_ref.shape[0]):
        du = lax.dot_general(dh_ref[...], wo_ref[cut, :], NT, preferred_element_type=jnp.float32)
        da_ref[:, cut] = (du * slope_ref[:, cut]).astype(jnp.bfloat16)


def low_grad(dh, wo, slope):
    return call(low_grad_kernel, "low_grad", None, [dh, wo, slope], [bf16(dh.shape[0], wo.shape[-2])])[0]


def pair_kernel(level, factor, order, a_cut, b_cut, where_ref, a_ref, an_ref, af_ref, b_ref, bn_ref, bf_ref, *rest):
    out_ref, right, both, slots, raw, sems = rest[-6:]
    rows = a_ref.shape[0]
    mine, theirs = pl.ds(0, rows), pl.ds(rows, rows)
    own = [
        pltpu.make_async_copy(a_ref.at[:, a_cut], both.at[mine, :], sems.at[2]),
        pltpu.make_async_copy(b_ref.at[:, b_cut], right.at[mine, :], sems.at[3]),
    ]
    if order:
        half = rows // 2
        own.append(pltpu.make_async_copy(bn_ref, raw.at[pl.ds(0, half), :], sems.at[6]))
        own.append(pltpu.make_async_copy(bf_ref, raw.at[pl.ds(half, half), :], sems.at[7]))
    for copy in own:
        copy.start()

    def take(a_mate, b_mate):
        copies = [pltpu.make_async_copy(a_mate.at[:, a_cut], both.at[theirs, :], sems.at[4])]
        if not order:
            copies.append(pltpu.make_async_copy(b_mate.at[:, b_cut], right.at[theirs, :], sems.at[5]))
        for copy in copies:
            copy.start()
        for copy in copies:
            copy.wait()

    @pl.when(where_ref[level] == 1)
    def _():
        take(an_ref, bn_ref)

    @pl.when(where_ref[level] != 1)
    def _():
        take(af_ref, bf_ref)

    for copy in own:
        copy.wait()
    if order:
        pick = places(order, rows, where_ref[3] ^ where_ref[level], where_ref[2])
        right[rows:, :] = jnp.dot(pick, raw[...], preferred_element_type=jnp.float32).astype(jnp.bfloat16)
    copies = []
    for i, cut in enumerate(cuts(both.shape[1], 2 * BLOCK)):
        slot = i % 2
        if i >= 2:
            copies[i - 2].wait()
        value = lax.dot_general(both[:, cut], right[...], TN, preferred_element_type=jnp.float32)
        slots[slot] = (value * factor).astype(jnp.bfloat16)
        copies.append(pltpu.make_async_copy(slots.at[slot], out_ref.at[0, level, cut, :], sems.at[slot]))
        copies[-1].start()
    for copy in copies[-2:]:
        copy.wait()


def pair_grad(where, a, a_mate, a_cut, b, b_mate, b_cut, level, before, order=""):
    rows, left, right = a.shape[0], a_cut.size, b_cut.size
    factor = -0.5 / rows**0.5
    arrays = [a, *a_mate, b, *b_mate]
    aliases = {}
    if before is not None:
        arrays.append(before)
        aliases = {len(arrays): 0}
    return pl.pallas_call(
        functools.partial(pair_kernel, level, factor, order, a_cut, b_cut),
        in_specs=[IN_SMEM] + [ANYWHERE] * len(arrays),
        out_specs=ANYWHERE,
        out_shape=bf16(1, 2, left, right),
        scratch_shapes=[
            pltpu.VMEM((2 * rows, right), jnp.bfloat16),
            pltpu.VMEM((2 * rows, left), jnp.bfloat16),
            pltpu.VMEM((2, min(2 * BLOCK, left), right), jnp.bfloat16),
            pltpu.VMEM((rows, right), jnp.bfloat16),
            pltpu.SemaphoreType.DMA((8,)),
        ],
        input_output_aliases=aliases,
        compiler_params=pltpu.CompilerParams(vmem_limit_bytes=56 * 1024 * 1024),
        cost_estimate=FREE,
        name="pair_grad",
    )(where, *arrays)


def dispatch(spread):
    got = lax.all_to_all(spread, ("path", "shard"), split_axis=0, concat_axis=0, tiled=True)
    return got.reshape(got.shape[0] * got.shape[1], got.shape[2])


def gather_shard(spread):
    got = lax.all_to_all(spread, "shard", split_axis=0, concat_axis=0, tiled=True)
    return got.reshape(got.shape[0] * got.shape[1], got.shape[2])


def scatter_shard(part):
    shards = lax.axis_size("shard")
    blocks = part.reshape(shards, part.shape[0] // shards, part.shape[1])
    return lax.all_to_all(blocks, "shard", split_axis=0, concat_axis=0, tiled=True)


def swap(value, axis, bit):
    return lax.ppermute(value, axis, [(i, i ^ bit) for i in range(lax.axis_size(axis))])


def join(*values):
    return lax.optimization_barrier(jnp.concatenate(values, axis=0))


def from_mate(values, *mates):
    paths = lax.axis_size("path")
    mates = mates if len(mates) == len(values) else mates * len(values)
    if paths == 4:
        nears = [swap(v, "path", 1) for v in values]
        sent = [jnp.where(mate == 3, near, v) for near, v, mate in zip(nears, values, mates)]
        return [[near, swap(v, "path", 2)] for near, v in zip(nears, sent)]
    me = lax.axis_index("path")
    pairs = []
    for value, mate in zip(values, mates):
        behind = (me - (me ^ mate)) % paths
        mine = value
        for shift in range(1, paths):
            got = lax.ppermute(value, "path", [(i, (i + shift) % paths) for i in range(paths)])
            value, mine = tie(value, jnp.where(behind == shift, got, mine))
        pairs.append([mine, mine])
    return pairs


def level_of(w, level, after):
    index, _ = tie(jnp.int32(level), after)
    return lax.dynamic_index_in_dim(w[0], index, 0, keepdims=False)


def body(tokens, routes, cotangent, gains, w_in, w_out, partners):
    paths = lax.axis_size("path")
    shards = lax.axis_size("shard")
    cubes = paths == 4 and shards == 8
    me = lax.axis_index("path")
    shard = lax.axis_index("shard")
    mate_low = partners[0, me] ^ me
    mate_high = partners[1, me] ^ me
    where = jnp.stack([mate_low, mate_high, shard, me])
    none = jnp.int32(0)
    gain = gains[0]
    routes = routes.reshape(-1)

    width, hidden = w_in.shape[2:]
    wide, first, second = pl.ds(0, width), pl.ds(0, hidden), pl.ds(hidden, hidden)

    spread = pack(none, routes, tokens, paths, shards)
    x = dispatch(spread)
    wi_low = level_of(w_in, 0, spread)
    if cubes:
        by_path = pack(me, routes, cotangent, paths, 0)
        rows_1 = join(by_path[0], *[swap(by_path[k], "path", k) for k in (1, 2, 3)])
        hop_1 = swap(rows_1, "shard", 4)
        wo_low = level_of(w_out, 0, rows_1)
        x, hop_1, where, mate_low, mate_high = tie(x, hop_1, where, mate_low, mate_high)
    else:
        wo_low = level_of(w_out, 0, spread)
    n1, u1, slope1, part_low = low_forward(x, gain, wi_low, wo_low)

    (n1_mate,) = from_mate([n1], mate_low)
    wi_high, wo_high = level_of(w_in, 1, n1_mate[0]), level_of(w_out, 1, n1_mate[0])
    got = scatter_shard(part_low)
    if cubes:
        rows_2 = join(rows_1, hop_1)
        hop_2 = swap(rows_2, "shard", 2)
        got, n1_mate[1], hop_2 = tie(got, n1_mate[1], hop_2)
    h_own, h_spread = settle(where, got, x)

    h = gather_shard(h_spread)
    if cubes:
        rows_4 = join(rows_2, hop_2)
        hop_3 = swap(rows_4, "shard", 1)
        (u1_mate, half_mate) = from_mate([u1, rows_4], mate_low, mate_high)
        dy, du2 = high_grad(where, join(rows_4, hop_3), wo_high, False)
        h, u1_mate[1], half_mate[1], du2 = tie(h, u1_mate[1], half_mate[1], du2)
    else:
        (u1_mate,) = from_mate([u1], mate_low)
        dy, du2 = high_grad(where, dispatch(pack(none, routes, cotangent, paths, shards)), wo_high, True)
    n2, f2, part_back = high_both(h, gain, wi_high, du2)

    (f2_mate,) = from_mate([f2], mate_high)
    wo_again = level_of(w_out, 0, f2_mate[0])
    got = scatter_shard(part_back)
    if cubes:
        half = jnp.where(mate_high == 1, *half_mate)
        hop_4 = swap(half, "shard", 1)
        got, f2_mate[1], hop_4 = tie(got, f2_mate[1], hop_4)
    dh_own, dh_spread = settle_back(where, got, dy, h_own, gain)

    dh = gather_shard(dh_spread)
    (n2_mate,) = from_mate([n2], mate_high)
    if cubes:
        delta_out = pair_grad(where, f2, f2_mate, first, dy, [half, hop_4], wide, 1, None, "dispatch")
        (dh_pair,) = from_mate([dh_own], mate_low)
        dh, n2_mate[1], delta_out = tie(dh, n2_mate[1], delta_out)
    da1 = low_grad(dh, wo_again, slope1)

    (da1_mate,) = from_mate([da1], mate_low)
    delta_in = pair_grad(where, n2, n2_mate, wide, f2, f2_mate, second, 1, None)
    if cubes:
        dh_piece, _ = tie(jnp.where(mate_low == 1, *dh_pair), da1)
        dh_half = join(dh_piece, *[swap(dh_piece, "shard", bit) for bit in (4, 2, 6)])
        dh_mate = [dh_half, swap(dh_half, "shard", 1)]
    else:
        (dh_mate,) = from_mate([dh], mate_low)
        (dy_mate,) = from_mate([dy], mate_high)
        delta_out = pair_grad(where, f2, f2_mate, first, dy, dy_mate, wide, 1, None)
    delta_in = pair_grad(where, n1, n1_mate, wide, da1, da1_mate, first, 0, delta_in)
    delta_out = pair_grad(where, u1, u1_mate, first, dh, dh_mate, wide, 0, delta_out, "gather" if cubes else "")
    return (delta_in, delta_out)


def solution(mesh):
    in_specs = (
        P(("path", "shard"), None),
        P(("path", "shard"), None),
        P(("path", "shard"), None),
        P("path", None, None),
        P("path", None, None, "shard"),
        P("path", None, "shard", None),
        P(),
    )
    out_specs = (P("path", None, None, "shard"), P("path", None, "shard", None))
    return jax.shard_map(body, mesh=mesh, in_specs=in_specs, out_specs=out_specs, check_vma=False)
```

```python
import functools

import jax
import jax.numpy as jnp
from jax import lax
from jax.experimental import pallas as pl
from jax.experimental.pallas import tpu as pltpu
from jax.sharding import PartitionSpec as P

SLOTS = 16
BLOCK = 256
ROOT = 0.7978845608028654
CUBE = 0.044715
NT = (((1,), (1,)), ((), ()))
TN = (((0,), (0,)), ((), ()))
PARAMS = pltpu.CompilerParams(vmem_limit_bytes=16 * 1024 * 1024)
SMALL = pltpu.CompilerParams(vmem_limit_bytes=56 * 1024 * 1024)
STREAM = pltpu.CompilerParams(vmem_limit_bytes=50 * 1024 * 1024)
IN_VMEM = pl.BlockSpec(memory_space=pltpu.VMEM)
IN_SMEM = pl.BlockSpec(memory_space=pltpu.SMEM)
ANYWHERE = pl.BlockSpec(memory_space=pl.ANY)
FREE = pl.CostEstimate(flops=0, bytes_accessed=0, transcendentals=0)


def bf16(*shape):
    return jax.ShapeDtypeStruct(shape, jnp.bfloat16)


def f32(*shape):
    return jax.ShapeDtypeStruct(shape, jnp.float32)


def cuts(size, step=BLOCK):
    step = min(step, size)
    return [pl.ds(start, step) for start in range(0, size, step)]


def tie(*values):
    return lax.optimization_barrier(values)


def call(kernel, name, where, arrays, outs):
    operands = [] if where is None else [where]
    return pl.pallas_call(
        kernel,
        in_specs=[IN_SMEM] * len(operands) + [IN_VMEM] * len(arrays),
        out_specs=[IN_VMEM] * len(outs),
        out_shape=outs,
        compiler_params=PARAMS,
        cost_estimate=FREE,
        name=name,
    )(*operands, *arrays)


def stream(kernel, name, where, arrays, weights, outs, buffers, copies):
    operands = [] if where is None else [where]
    return pl.pallas_call(
        kernel,
        in_specs=[IN_SMEM] * len(operands) + [IN_VMEM] * len(arrays) + [ANYWHERE] * len(weights),
        out_specs=[IN_VMEM] * len(outs),
        out_shape=outs,
        scratch_shapes=[pltpu.VMEM(shape, jnp.bfloat16) for shape in buffers] + [pltpu.SemaphoreType.DMA((copies,))],
        compiler_params=STREAM,
        cost_estimate=FREE,
        name=name,
    )(*operands, *arrays, *weights)


def bring(w_ref, level, buffer, sems, first, along):
    pieces = []
    for i, cut in enumerate(cuts(buffer.shape[along])):
        source = w_ref.at[0, level, cut, :] if along == 0 else w_ref.at[0, level, :, cut]
        target = buffer.at[cut, :] if along == 0 else buffer.at[:, cut]
        copy = pltpu.make_async_copy(source, target, sems.at[first + i])
        copy.start()
        pieces.append((cut, copy))
    return pieces


def norm_value(v, gain):
    return v * lax.rsqrt(jnp.mean(v * v, axis=-1, keepdims=True) + 1e-05) * gain.astype(jnp.float32)


def gelu_both(a):
    t = jnp.tanh(ROOT * (a + CUBE * (a * a * a)))
    half = 0.5 * (1.0 + t)
    slope = half + 0.5 * a * (1.0 - t * t) * (ROOT * (1.0 + (3.0 * CUBE) * (a * a)))
    return a * half, slope


def slots_of_rows(routes_ref, cap, flip):
    count = routes_ref.shape[0]
    down = lax.broadcasted_iota(jnp.int32, (count, count), 0)
    along = lax.broadcasted_iota(jnp.int32, (count, count), 1)
    route_down = jnp.zeros((count, count), jnp.int32)
    route_along = jnp.zeros((count, count), jnp.int32)
    for r in range(count):
        route = routes_ref[r]
        route_down = jnp.where(down == r, route, route_down)
        route_along = jnp.where(along == r, route, route_along)
    earlier = jnp.where((route_down == route_along) & (down < along), 1, 0)
    rank = jnp.sum(earlier, axis=0, keepdims=True)
    return (route_along[0:1, :] ^ flip) * cap + rank


def pack_kernel(copies, flip_ref, routes_ref, rows_ref, *out_refs):
    count = routes_ref.shape[0]
    cap = out_refs[0].shape[-2]
    slots = slots_of_rows(routes_ref, cap, flip_ref[0])
    for group in range(SLOTS // cap):
        want = group * cap + lax.broadcasted_iota(jnp.int32, (cap, count), 0)
        pick = (want == slots).astype(jnp.float32).astype(jnp.bfloat16)
        value = jnp.dot(pick, rows_ref[...], preferred_element_type=jnp.float32).astype(jnp.bfloat16)
        if copies == 0:
            out_refs[group][...] = value
        for copy in range(copies):
            out_refs[0][group * copies + copy] = value


def pack(flip, routes, rows, paths, copies):
    cap, width = SLOTS // paths, rows.shape[1]
    outs = [bf16(paths * copies, cap, width)] if copies else [bf16(cap, width)] * paths
    got = pl.pallas_call(
        functools.partial(pack_kernel, copies),
        in_specs=[IN_SMEM, IN_SMEM, IN_VMEM],
        out_specs=[IN_VMEM] * len(outs),
        out_shape=outs,
        compiler_params=SMALL,
        cost_estimate=FREE,
        name="pack",
    )(flip.reshape(1), routes, rows)
    return got[0] if copies else got


def settle_kernel(where_ref, got_ref, x_ref, own_ref, spread_ref):
    count, rows, _ = got_ref.shape
    total = x_ref[pl.ds(pl.multiple_of(where_ref[2] * rows, rows), rows), :].astype(jnp.float32)
    for i in range(count):
        total += got_ref[i].astype(jnp.float32)
    total = total.astype(jnp.bfloat16)
    own_ref[...] = total
    for i in range(count):
        spread_ref[i] = total


def settle(where, got, x):
    count, rows, width = got.shape
    return call(settle_kernel, "settle", where, [got, x], [bf16(rows, width), bf16(count, rows, width)])


def settle_back_kernel(where_ref, got_ref, dy_ref, h_ref, gain_ref, own_ref, spread_ref):
    count, rows, _ = got_ref.shape
    grad = got_ref[0].astype(jnp.float32)
    for i in range(1, count):
        grad += got_ref[i].astype(jnp.float32)
    grad = grad * gain_ref[1:2, :].astype(jnp.float32)
    h = h_ref[...].astype(jnp.float32)
    scale = lax.rsqrt(jnp.mean(h * h, axis=-1, keepdims=True) + 1e-05)
    unit = h * scale
    pull = scale * (grad - unit * jnp.mean(grad * unit, axis=-1, keepdims=True))
    dy = dy_ref[pl.ds(pl.multiple_of(where_ref[2] * rows, rows), rows), :].astype(jnp.float32)
    total = (dy + pull).astype(jnp.bfloat16)
    own_ref[...] = total
    for i in range(count):
        spread_ref[i] = total


def settle_back(where, got, dy, h_own, gains):
    count, rows, width = got.shape
    outs = [bf16(rows, width), bf16(count, rows, width)]
    return call(settle_back_kernel, "settle_back", where, [got, dy, h_own, gains], outs)


def low_kernel(x_ref, gain_ref, wi_ref, wo_ref, n_ref, u_ref, slope_ref, part_ref, wi, wo, sems):
    into = bring(wi_ref, 0, wi, sems, 0, 1)
    n_ref[...] = norm_value(x_ref[...].astype(jnp.float32), gain_ref[0:1, :]).astype(jnp.bfloat16)
    for i, (cut, copy) in enumerate(into):
        copy.wait()
        if i == 0:
            out_of = bring(wo_ref, 0, wo, sems, len(into), 1)
        a = jnp.dot(n_ref[...], wi[:, cut], preferred_element_type=jnp.float32)
        u, slope = gelu_both(a)
        u_ref[:, cut] = u.astype(jnp.bfloat16)
        slope_ref[:, cut] = slope
    for cut, copy in out_of:
        copy.wait()
        part = jnp.dot(u_ref[...], wo[:, cut], preferred_element_type=jnp.float32)
        part_ref[:, cut] = part.astype(jnp.bfloat16)


def low_forward(x, gains, w_in, w_out):
    rows, width = x.shape
    hidden = w_in.shape[3]
    outs = [bf16(rows, width), bf16(rows, hidden), f32(rows, hidden), bf16(rows, width)]
    copies = len(cuts(hidden)) + len(cuts(width))
    buffers = [(width, hidden), (hidden, width)]
    return stream(low_kernel, "low_forward", None, [x, gains], [w_in, w_out], outs, buffers, copies)


def high_kernel(h_ref, gain_ref, du_ref, wi_ref, n_ref, pair_ref, part_ref, wi, sems):
    into = bring(wi_ref, 1, wi, sems, 0, 1)
    hidden = wi.shape[1]
    n_ref[...] = norm_value(h_ref[...].astype(jnp.float32), gain_ref[1:2, :]).astype(jnp.bfloat16)
    for cut, copy in into:
        copy.wait()
        a = jnp.dot(n_ref[...], wi[:, cut], preferred_element_type=jnp.float32)
        u, slope = gelu_both(a)
        pair_ref[:, cut] = u.astype(jnp.bfloat16)
        pair_ref[:, pl.ds(hidden + cut.start, cut.size)] = (slope * du_ref[:, cut]).astype(jnp.bfloat16)
    for cut in cuts(wi.shape[0]):
        part = lax.dot_general(pair_ref[:, hidden:], wi[cut, :], NT, preferred_element_type=jnp.float32)
        part_ref[:, cut] = part.astype(jnp.bfloat16)


def high_both(h, gains, w_in, du):
    rows, width = h.shape
    hidden = w_in.shape[3]
    outs = [bf16(rows, width), bf16(rows, 2 * hidden), bf16(rows, width)]
    return stream(
        high_kernel, "high_both", None, [h, gains, du], [w_in], outs, [(width, hidden)], len(cuts(hidden))
    )


def places(order, rows, path, shard):
    to = lax.broadcasted_iota(jnp.int32, (rows, rows), 0)
    source = lax.broadcasted_iota(jnp.int32, (rows, rows), 1)
    if order == "dispatch":
        far = ((to >> 2) & 7) ^ shard
        block = ((far & 1) << 2) | (far & 2) | (far >> 2)
        wanted = block * 16 + ((to >> 5) ^ path) * 4 + (to & 3)
    else:
        far = (to >> 4) ^ shard
        block = ((far & 1) << 2) | (far & 2) | (far >> 2)
        wanted = block * 16 + (to & 15)
    return (source == wanted).astype(jnp.float32).astype(jnp.bfloat16)


def high_grad_kernel(ordered, where_ref, raw_ref, wo_ref, dy_ref, du_ref, wo, sems):
    pieces = bring(wo_ref, 1, wo, sems, 0, 0)
    if ordered:
        dy_ref[...] = raw_ref[...]
    else:
        pick = places("dispatch", raw_ref.shape[0], where_ref[3], where_ref[2])
        dy_ref[...] = jnp.dot(pick, raw_ref[...], preferred_element_type=jnp.float32).astype(jnp.bfloat16)
    for cut, copy in pieces:
        copy.wait()
        du_ref[:, cut] = lax.dot_general(dy_ref[...], wo[cut, :], NT, preferred_element_type=jnp.float32)


def high_grad(where, raw, w_out, ordered):
    rows, width = raw.shape
    hidden = w_out.shape[2]
    outs = [bf16(rows, width), f32(rows, hidden)]
    kernel = functools.partial(high_grad_kernel, ordered)
    return stream(kernel, "high_grad", where, [raw], [w_out], outs, [(hidden, width)], len(cuts(hidden)))


def low_grad_kernel(dh_ref, slope_ref, wo_ref, da_ref, wo, sems):
    for cut, copy in bring(wo_ref, 0, wo, sems, 0, 0):
        copy.wait()
        du = lax.dot_general(dh_ref[...], wo[cut, :], NT, preferred_element_type=jnp.float32)
        da_ref[:, cut] = (du * slope_ref[:, cut]).astype(jnp.bfloat16)


def low_grad(dh, w_out, slope):
    rows, width = dh.shape
    hidden = w_out.shape[2]
    outs = [bf16(rows, hidden)]
    return stream(low_grad_kernel, "low_grad", None, [dh, slope], [w_out], outs, [(hidden, width)], len(cuts(hidden)))[0]


def pair_kernel(level, factor, order, a_cut, b_cut, where_ref, a_ref, an_ref, af_ref, b_ref, bn_ref, bf_ref, *rest):
    out_ref, right, both, slots, raw, sems = rest[-6:]
    rows = a_ref.shape[0]
    mine, theirs = pl.ds(0, rows), pl.ds(rows, rows)
    own = [
        pltpu.make_async_copy(a_ref.at[:, a_cut], both.at[mine, :], sems.at[2]),
        pltpu.make_async_copy(b_ref.at[:, b_cut], right.at[mine, :], sems.at[3]),
    ]
    if order:
        half = rows // 2
        own.append(pltpu.make_async_copy(bn_ref, raw.at[pl.ds(0, half), :], sems.at[6]))
        own.append(pltpu.make_async_copy(bf_ref, raw.at[pl.ds(half, half), :], sems.at[7]))
    for copy in own:
        copy.start()

    def take(a_mate, b_mate):
        copies = [pltpu.make_async_copy(a_mate.at[:, a_cut], both.at[theirs, :], sems.at[4])]
        if not order:
            copies.append(pltpu.make_async_copy(b_mate.at[:, b_cut], right.at[theirs, :], sems.at[5]))
        for copy in copies:
            copy.start()
        for copy in copies:
            copy.wait()

    @pl.when(where_ref[level] == 1)
    def _():
        take(an_ref, bn_ref)

    @pl.when(where_ref[level] != 1)
    def _():
        take(af_ref, bf_ref)

    for copy in own:
        copy.wait()
    if order:
        pick = places(order, rows, where_ref[3] ^ where_ref[level], where_ref[2])
        right[rows:, :] = jnp.dot(pick, raw[...], preferred_element_type=jnp.float32).astype(jnp.bfloat16)
    copies = []
    for i, cut in enumerate(cuts(both.shape[1], 2 * BLOCK)):
        slot = i % 2
        if i >= 2:
            copies[i - 2].wait()
        value = lax.dot_general(both[:, cut], right[...], TN, preferred_element_type=jnp.float32)
        slots[slot] = (value * factor).astype(jnp.bfloat16)
        copies.append(pltpu.make_async_copy(slots.at[slot], out_ref.at[0, level, cut, :], sems.at[slot]))
        copies[-1].start()
    for copy in copies[-2:]:
        copy.wait()


def pair_grad(where, a, a_mate, a_cut, b, b_mate, b_cut, level, before, order=""):
    rows, left, right = a.shape[0], a_cut.size, b_cut.size
    factor = -0.5 / rows**0.5
    arrays = [a, *a_mate, b, *b_mate]
    aliases = {}
    if before is not None:
        arrays.append(before)
        aliases = {len(arrays): 0}
    return pl.pallas_call(
        functools.partial(pair_kernel, level, factor, order, a_cut, b_cut),
        in_specs=[IN_SMEM] + [ANYWHERE] * len(arrays),
        out_specs=ANYWHERE,
        out_shape=bf16(1, 2, left, right),
        scratch_shapes=[
            pltpu.VMEM((2 * rows, right), jnp.bfloat16),
            pltpu.VMEM((2 * rows, left), jnp.bfloat16),
            pltpu.VMEM((2, min(2 * BLOCK, left), right), jnp.bfloat16),
            pltpu.VMEM((rows, right), jnp.bfloat16),
            pltpu.SemaphoreType.DMA((8,)),
        ],
        input_output_aliases=aliases,
        compiler_params=pltpu.CompilerParams(vmem_limit_bytes=56 * 1024 * 1024),
        cost_estimate=FREE,
        name="pair_grad",
    )(where, *arrays)


def dispatch(spread):
    got = lax.all_to_all(spread, ("path", "shard"), split_axis=0, concat_axis=0, tiled=True)
    return got.reshape(got.shape[0] * got.shape[1], got.shape[2])


def gather_shard(spread):
    got = lax.all_to_all(spread, "shard", split_axis=0, concat_axis=0, tiled=True)
    return got.reshape(got.shape[0] * got.shape[1], got.shape[2])


def scatter_shard(part):
    shards = lax.axis_size("shard")
    blocks = part.reshape(shards, part.shape[0] // shards, part.shape[1])
    return lax.all_to_all(blocks, "shard", split_axis=0, concat_axis=0, tiled=True)


def swap(value, axis, bit):
    return lax.ppermute(value, axis, [(i, i ^ bit) for i in range(lax.axis_size(axis))])


def join(*values):
    return lax.optimization_barrier(jnp.concatenate(values, axis=0))


def from_mate(values, *mates):
    paths = lax.axis_size("path")
    mates = mates if len(mates) == len(values) else mates * len(values)
    if paths == 4:
        nears = [swap(v, "path", 1) for v in values]
        sent = [jnp.where(mate == 3, near, v) for near, v, mate in zip(nears, values, mates)]
        return [[near, swap(v, "path", 2)] for near, v in zip(nears, sent)]
    me = lax.axis_index("path")
    pairs = []
    for value, mate in zip(values, mates):
        behind = (me - (me ^ mate)) % paths
        mine = value
        for shift in range(1, paths):
            got = lax.ppermute(value, "path", [(i, (i + shift) % paths) for i in range(paths)])
            value, mine = tie(value, jnp.where(behind == shift, got, mine))
        pairs.append([mine, mine])
    return pairs


def body(tokens, routes, cotangent, gains, w_in, w_out, partners):
    paths = lax.axis_size("path")
    shards = lax.axis_size("shard")
    cubes = paths == 4 and shards == 8
    me = lax.axis_index("path")
    shard = lax.axis_index("shard")
    mate_low = partners[0, me] ^ me
    mate_high = partners[1, me] ^ me
    where = jnp.stack([mate_low, mate_high, shard, me])
    none = jnp.int32(0)
    gain = gains[0]
    routes = routes.reshape(-1)

    width, hidden = w_in.shape[2:]
    wide, first, second = pl.ds(0, width), pl.ds(0, hidden), pl.ds(hidden, hidden)

    spread = pack(none, routes, tokens, paths, shards)
    x = dispatch(spread)
    if cubes:
        by_path = pack(me, routes, cotangent, paths, 0)
        rows_1 = join(by_path[0], *[swap(by_path[k], "path", k) for k in (1, 2, 3)])
        hop_1 = swap(rows_1, "shard", 4)
        x, hop_1, where, mate_low, mate_high = tie(x, hop_1, where, mate_low, mate_high)
    n1, u1, slope1, part_low = low_forward(x, gain, w_in, w_out)

    (n1_mate,) = from_mate([n1], mate_low)
    got = scatter_shard(part_low)
    if cubes:
        rows_2 = join(rows_1, hop_1)
        hops = [swap(rows_2, "shard", bit) for bit in (2, 1, 3)]
        got, n1_mate[1], *hops = tie(got, n1_mate[1], *hops)
    h_own, h_spread = settle(where, got, x)

    h = gather_shard(h_spread)
    (u1_mate,) = from_mate([u1], mate_low)
    if cubes:
        hops[0], _ = tie(hops[0], u1_mate[0])
        rows_4 = join(rows_2, hops[0])
        (half_mate,) = from_mate([rows_4], mate_high)
        dy, du2 = high_grad(where, join(rows_4, *hops[1:]), w_out, False)
        h, u1_mate[1], half_mate[1], du2 = tie(h, u1_mate[1], half_mate[1], du2)
    else:
        dy, du2 = high_grad(where, dispatch(pack(none, routes, cotangent, paths, shards)), w_out, True)
    n2, f2, part_back = high_both(h, gain, w_in, du2)

    (f2_mate,) = from_mate([f2], mate_high)
    got = scatter_shard(part_back)
    if cubes:
        half = jnp.where(mate_high == 1, *half_mate)
        hop_4 = swap(half, "shard", 1)
        got, f2_mate[1], hop_4 = tie(got, f2_mate[1], hop_4)
    dh_own, dh_spread = settle_back(where, got, dy, h_own, gain)

    dh = gather_shard(dh_spread)
    (n2_mate,) = from_mate([n2], mate_high)
    if cubes:
        delta_out = pair_grad(where, f2, f2_mate, first, dy, [half, hop_4], wide, 1, None, "dispatch")
        dh_own, _ = tie(dh_own, n2_mate[0])
        (dh_pair,) = from_mate([dh_own], mate_low)
        dh_piece = jnp.where(mate_low == 1, *dh_pair)
        pieces = [swap(dh_piece, "shard", bit) for bit in (4, 2, 6)]
        dh, n2_mate[1], delta_out, dh_piece = tie(dh, n2_mate[1], delta_out, dh_piece)
    da1 = low_grad(dh, w_out, slope1)

    if cubes:
        da1, *pieces = tie(da1, *pieces)
    (da1_mate,) = from_mate([da1], mate_low)
    delta_in = pair_grad(where, n2, n2_mate, wide, f2, f2_mate, second, 1, None)
    if cubes:
        dh_half = join(dh_piece, *pieces)
        dh_mate = [dh_half, swap(dh_half, "shard", 1)]
    else:
        (dh_mate,) = from_mate([dh], mate_low)
        (dy_mate,) = from_mate([dy], mate_high)
        delta_out = pair_grad(where, f2, f2_mate, first, dy, dy_mate, wide, 1, None)
    delta_in = pair_grad(where, n1, n1_mate, wide, da1, da1_mate, first, 0, delta_in)
    delta_out = pair_grad(where, u1, u1_mate, first, dh, dh_mate, wide, 0, delta_out, "gather" if cubes else "")
    return (delta_in, delta_out)


def solution(mesh):
    in_specs = (
        P(("path", "shard"), None),
        P(("path", "shard"), None),
        P(("path", "shard"), None),
        P("path", None, None),
        P("path", None, None, "shard"),
        P("path", None, "shard", None),
        P(),
    )
    out_specs = (P("path", None, None, "shard"), P("path", None, "shard", None))
    return jax.shard_map(body, mesh=mesh, in_specs=in_specs, out_specs=out_specs, check_vma=False)
```

```python
import functools

import jax
import jax.numpy as jnp
from jax import lax
from jax.experimental import pallas as pl
from jax.experimental.pallas import tpu as pltpu
from jax.sharding import PartitionSpec as P

SLOTS = 16
BLOCK = 256
ROOT = 0.7978845608028654
CUBE = 0.044715
NT = (((1,), (1,)), ((), ()))
TN = (((0,), (0,)), ((), ()))
PARAMS = pltpu.CompilerParams(vmem_limit_bytes=16 * 1024 * 1024)
SMALL = pltpu.CompilerParams(vmem_limit_bytes=56 * 1024 * 1024)
STREAM = pltpu.CompilerParams(vmem_limit_bytes=50 * 1024 * 1024)
IN_VMEM = pl.BlockSpec(memory_space=pltpu.VMEM)
IN_HBM = pl.BlockSpec(memory_space=pltpu.HBM)
IN_SMEM = pl.BlockSpec(memory_space=pltpu.SMEM)
ANYWHERE = pl.BlockSpec(memory_space=pl.ANY)
FREE = pl.CostEstimate(flops=0, bytes_accessed=0, transcendentals=0)


def bf16(*shape):
    return jax.ShapeDtypeStruct(shape, jnp.bfloat16)


def f32(*shape):
    return jax.ShapeDtypeStruct(shape, jnp.float32)


def cuts(size, step=BLOCK):
    step = min(step, size)
    return [pl.ds(start, step) for start in range(0, size, step)]


def tie(*values):
    return lax.optimization_barrier(values)


def call(kernel, name, where, arrays, outs):
    operands = [] if where is None else [where]
    return pl.pallas_call(
        kernel,
        in_specs=[IN_SMEM] * len(operands) + [IN_VMEM] * len(arrays),
        out_specs=[IN_VMEM] * len(outs),
        out_shape=outs,
        compiler_params=PARAMS,
        cost_estimate=FREE,
        name=name,
    )(*operands, *arrays)


def stream(kernel, name, where, arrays, weights, outs, buffers, copies, away=0):
    operands = [] if where is None else [where]
    return pl.pallas_call(
        kernel,
        in_specs=[IN_SMEM] * len(operands) + [IN_VMEM] * len(arrays) + [ANYWHERE] * len(weights),
        out_specs=[IN_VMEM] * (len(outs) - away) + [IN_HBM] * away,
        out_shape=outs,
        scratch_shapes=[pltpu.VMEM(shape, jnp.bfloat16) for shape in buffers] + [pltpu.SemaphoreType.DMA((copies,))],
        compiler_params=STREAM,
        cost_estimate=FREE,
        name=name,
    )(*operands, *arrays, *weights)


def bring(w_ref, level, buffer, sems, first, along):
    pieces = []
    for i, cut in enumerate(cuts(buffer.shape[along])):
        source = w_ref.at[0, level, cut, :] if along == 0 else w_ref.at[0, level, :, cut]
        target = buffer.at[cut, :] if along == 0 else buffer.at[:, cut]
        copy = pltpu.make_async_copy(source, target, sems.at[first + i])
        copy.start()
        pieces.append((cut, copy))
    return pieces


def norm_value(v, gain):
    return v * lax.rsqrt(jnp.mean(v * v, axis=-1, keepdims=True) + 1e-05) * gain.astype(jnp.float32)


def gelu_both(a):
    t = jnp.tanh(ROOT * (a + CUBE * (a * a * a)))
    half = 0.5 * (1.0 + t)
    slope = half + 0.5 * a * (1.0 - t * t) * (ROOT * (1.0 + (3.0 * CUBE) * (a * a)))
    return a * half, slope


def slots_of_rows(routes_ref, cap, flip):
    count = routes_ref.shape[0]
    down = lax.broadcasted_iota(jnp.int32, (count, count), 0)
    along = lax.broadcasted_iota(jnp.int32, (count, count), 1)
    route_down = jnp.zeros((count, count), jnp.int32)
    route_along = jnp.zeros((count, count), jnp.int32)
    for r in range(count):
        route = routes_ref[r]
        route_down = jnp.where(down == r, route, route_down)
        route_along = jnp.where(along == r, route, route_along)
    earlier = jnp.where((route_down == route_along) & (down < along), 1, 0)
    rank = jnp.sum(earlier, axis=0, keepdims=True)
    return (route_along[0:1, :] ^ flip) * cap + rank


def pack_kernel(copies, flip_ref, routes_ref, rows_ref, *out_refs):
    count = routes_ref.shape[0]
    cap = out_refs[0].shape[-2]
    slots = slots_of_rows(routes_ref, cap, flip_ref[0])
    for group in range(SLOTS // cap):
        want = group * cap + lax.broadcasted_iota(jnp.int32, (cap, count), 0)
        pick = (want == slots).astype(jnp.float32).astype(jnp.bfloat16)
        value = jnp.dot(pick, rows_ref[...], preferred_element_type=jnp.float32).astype(jnp.bfloat16)
        if copies == 0:
            out_refs[group][...] = value
        for copy in range(copies):
            out_refs[0][group * copies + copy] = value


def pack(flip, routes, rows, paths, copies):
    cap, width = SLOTS // paths, rows.shape[1]
    outs = [bf16(paths * copies, cap, width)] if copies else [bf16(cap, width)] * paths
    got = pl.pallas_call(
        functools.partial(pack_kernel, copies),
        in_specs=[IN_SMEM, IN_SMEM, IN_VMEM],
        out_specs=[IN_VMEM] * len(outs),
        out_shape=outs,
        compiler_params=SMALL,
        cost_estimate=FREE,
        name="pack",
    )(flip.reshape(1), routes, rows)
    return got[0] if copies else got


def settle_kernel(where_ref, got_ref, x_ref, own_ref, spread_ref):
    count, rows, _ = got_ref.shape
    total = x_ref[pl.ds(pl.multiple_of(where_ref[2] * rows, rows), rows), :].astype(jnp.float32)
    for i in range(count):
        total += got_ref[i].astype(jnp.float32)
    total = total.astype(jnp.bfloat16)
    own_ref[...] = total
    for i in range(count):
        spread_ref[i] = total


def settle(where, got, x):
    count, rows, width = got.shape
    return call(settle_kernel, "settle", where, [got, x], [bf16(rows, width), bf16(count, rows, width)])


def pull_back(dy, h, gain, grad):
    grad = grad * gain.astype(jnp.float32)
    h = h.astype(jnp.float32)
    scale = lax.rsqrt(jnp.mean(h * h, axis=-1, keepdims=True) + 1e-05)
    unit = h * scale
    pull = scale * (grad - unit * jnp.mean(grad * unit, axis=-1, keepdims=True))
    return (dy.astype(jnp.float32) + pull).astype(jnp.bfloat16)


def settle_back_kernel(where_ref, got_ref, dy_ref, h_ref, gain_ref, own_ref, spread_ref):
    count, rows, _ = got_ref.shape
    grad = got_ref[0].astype(jnp.float32)
    for i in range(1, count):
        grad += got_ref[i].astype(jnp.float32)
    dy = dy_ref[pl.ds(pl.multiple_of(where_ref[2] * rows, rows), rows), :]
    total = pull_back(dy, h_ref[...], gain_ref[1:2, :], grad)
    own_ref[...] = total
    for i in range(count):
        spread_ref[i] = total


def settle_back(where, got, dy, h_own, gains):
    count, rows, width = got.shape
    outs = [bf16(rows, width), bf16(count, rows, width)]
    return call(settle_back_kernel, "settle_back", where, [got, dy, h_own, gains], outs)


def half_kernel(where_ref, keep_ref, got_ref, mine_ref, *rest):
    gives, total = rest[:-1], rest[-1]
    total[...] = keep_ref[...].astype(jnp.float32) + got_ref[...].astype(jnp.float32)
    z = where_ref[2] >> 1
    mine_ref[...] = total[z]
    for step, give_ref in enumerate(gives):
        give_ref[...] = total[z ^ (step + 1)].astype(jnp.bfloat16)


def half_sums(where, keep, got):
    groups, rows, width = keep.shape
    return pl.pallas_call(
        half_kernel,
        in_specs=[IN_SMEM] + [IN_VMEM] * 2,
        out_specs=[IN_VMEM] * groups,
        out_shape=[f32(rows, width)] + [bf16(rows, width)] * (groups - 1),
        scratch_shapes=[pltpu.VMEM(keep.shape, jnp.float32)],
        compiler_params=PARAMS,
        cost_estimate=FREE,
        name="half_sums",
    )(where, keep, got)


def last_kernel(x_ref, mine_ref, *rest):
    total = x_ref[...].astype(jnp.float32) + mine_ref[...]
    for got_ref in rest[:-1]:
        total += got_ref[...].astype(jnp.float32)
    rest[-1][...] = total.astype(jnp.bfloat16)


def last_sums(x_own, mine, got):
    return call(last_kernel, "last_sums", None, [x_own, mine, *got], [bf16(*x_own.shape)])[0]


def last_back_kernel(dy_ref, h_ref, gain_ref, mine_ref, *rest):
    grad = mine_ref[...]
    for got_ref in rest[:-1]:
        grad += got_ref[...].astype(jnp.float32)
    rest[-1][...] = pull_back(dy_ref[...], h_ref[...], gain_ref[1:2, :], grad)


def last_back(dy_own, h_own, gains, mine, got):
    return call(last_back_kernel, "last_back", None, [dy_own, h_own, gains, mine, *got], [bf16(*h_own.shape)])[0]


def low_kernel(steps, where_ref, x_ref, gain_ref, wi_ref, wo_ref, n_ref, u_ref, slope_ref, *rest):
    if steps:
        own_ref, keep_ref, give_ref, wi, wo, part_ref, sems = rest
        own_ref[...] = x_ref[pl.ds(pl.multiple_of(where_ref[2] * SLOTS, SLOTS), SLOTS), :]
    else:
        part_ref, wi, wo, sems = rest
    into = bring(wi_ref, 0, wi, sems, 0, 1)
    n_ref[...] = norm_value(x_ref[...].astype(jnp.float32), gain_ref[0:1, :]).astype(jnp.bfloat16)
    for i, (cut, copy) in enumerate(into):
        copy.wait()
        if i == 0:
            out_of = bring(wo_ref, 0, wo, sems, len(into), 1)
        a = jnp.dot(n_ref[...], wi[:, cut], preferred_element_type=jnp.float32)
        u, slope = gelu_both(a)
        u_ref[:, cut] = u.astype(jnp.bfloat16)
        slope_ref[:, cut] = slope
    for cut, copy in out_of:
        copy.wait()
        part = jnp.dot(u_ref[...], wo[:, cut], preferred_element_type=jnp.float32)
        part_ref[:, cut] = part.astype(jnp.bfloat16)
    if steps:
        split_rows(part_ref, where_ref[2], keep_ref, give_ref)


def split_rows(part_ref, shard, keep_ref, give_ref):
    groups = part_ref.shape[0] // (2 * SLOTS)
    for y in range(2):

        @pl.when((shard & 1) == y)
        def _():
            for z in range(groups):
                start = z * 2 * SLOTS
                keep_ref[z] = part_ref[start + y * SLOTS : start + (y + 1) * SLOTS, :]
                give_ref[z] = part_ref[start + (1 - y) * SLOTS : start + (2 - y) * SLOTS, :]


def place_rows(half_ref, other_ref, shard, out_ref):
    for step in range(half_ref.shape[0] // SLOTS):
        for flip, source in enumerate((half_ref, other_ref)):
            start = pl.multiple_of((shard ^ (2 * step) ^ flip) * SLOTS, SLOTS)
            out_ref[pl.ds(start, SLOTS), :] = source[step * SLOTS : (step + 1) * SLOTS, :]


def low_forward(where, x, gains, w_in, w_out, steps):
    rows, width = x.shape
    hidden = w_in.shape[3]
    outs = [bf16(rows, width), bf16(rows, hidden), f32(rows, hidden)]
    buffers = [(width, hidden), (hidden, width)]
    if steps:
        outs += [bf16(SLOTS, width)] + [bf16(rows // (2 * SLOTS), SLOTS, width)] * 2
        buffers.append((rows, width))
    else:
        outs.append(bf16(rows, width))
    copies = len(cuts(hidden)) + len(cuts(width))
    return stream(functools.partial(low_kernel, steps), "low_forward", where, [x, gains], [w_in, w_out], outs, buffers, copies)


def high_kernel(steps, where_ref, *refs):
    if steps:
        half_ref, other_ref, gain_ref, du_ref, wi_ref, n_ref, u_ref, da_ref, keep_ref, give_ref, wi, h_ref, part_ref, sems = refs
    else:
        h_ref, gain_ref, du_ref, wi_ref, n_ref, u_ref, da_ref, part_ref, wi, sems = refs
    into = bring(wi_ref, 1, wi, sems, 0, 1)
    if steps:
        place_rows(half_ref, other_ref, where_ref[2], h_ref)
    n_ref[...] = norm_value(h_ref[...].astype(jnp.float32), gain_ref[1:2, :]).astype(jnp.bfloat16)
    for cut, copy in into:
        copy.wait()
        a = jnp.dot(n_ref[...], wi[:, cut], preferred_element_type=jnp.float32)
        u, slope = gelu_both(a)
        u_ref[:, cut] = u.astype(jnp.bfloat16)
        da_ref[:, cut] = (slope * du_ref[:, cut]).astype(jnp.bfloat16)
    for cut in cuts(wi.shape[0]):
        part = lax.dot_general(da_ref[...], wi[cut, :], NT, preferred_element_type=jnp.float32)
        part_ref[:, cut] = part.astype(jnp.bfloat16)
    if steps:
        split_rows(part_ref, where_ref[2], keep_ref, give_ref)


def high_both(where, h, gains, w_in, du, steps):
    rows, width = du.shape[0], gains.shape[1]
    hidden = w_in.shape[3]
    outs = [bf16(rows, width), bf16(rows, hidden), bf16(rows, hidden)]
    buffers = [(width, hidden)]
    if steps:
        outs += [bf16(rows // (2 * SLOTS), SLOTS, width)] * 2
        buffers += [(rows, width)] * 2
    else:
        outs.append(bf16(rows, width))
    kernel = functools.partial(high_kernel, steps)
    return stream(kernel, "high_both", where, [*h, gains, du], [w_in], outs, buffers, len(cuts(hidden)))


def places(order, rows, path, shard):
    to = lax.broadcasted_iota(jnp.int32, (rows, rows), 0)
    source = lax.broadcasted_iota(jnp.int32, (rows, rows), 1)
    if order == "dispatch":
        far = ((to >> 2) & 7) ^ shard
        block = ((far & 1) << 2) | (far & 2) | (far >> 2)
        wanted = block * 16 + ((to >> 5) ^ path) * 4 + (to & 3)
    else:
        far = (to >> 4) ^ shard
        block = ((far & 1) << 2) | (far & 2) | (far >> 2)
        wanted = block * 16 + (to & 15)
    return (source == wanted).astype(jnp.float32).astype(jnp.bfloat16)


def high_grad_kernel(ordered, where_ref, raw_ref, wo_ref, own_ref, du_ref, out_ref, wo, dy_ref, sems):
    pieces = bring(wo_ref, 1, wo, sems, 0, 0)
    if ordered:
        dy_ref[...] = raw_ref[...]
    else:
        pick = places("dispatch", raw_ref.shape[0], where_ref[3], where_ref[2])
        dy_ref[...] = jnp.dot(pick, raw_ref[...], preferred_element_type=jnp.float32).astype(jnp.bfloat16)
    out = pltpu.make_async_copy(dy_ref, out_ref, sems.at[len(pieces)])
    out.start()
    own_ref[...] = dy_ref[pl.ds(pl.multiple_of(where_ref[2] * SLOTS, SLOTS), SLOTS), :]
    for cut, copy in pieces:
        copy.wait()
        du_ref[:, cut] = lax.dot_general(dy_ref[...], wo[cut, :], NT, preferred_element_type=jnp.float32)
    out.wait()


def high_grad(where, raw, w_out, ordered):
    rows, width = raw.shape
    hidden = w_out.shape[2]
    outs = [bf16(SLOTS, width), f32(rows, hidden), bf16(rows, width)]
    kernel = functools.partial(high_grad_kernel, ordered)
    buffers = [(hidden, width), (rows, width)]
    return stream(kernel, "high_grad", where, [raw], [w_out], outs, buffers, len(cuts(hidden)) + 1, 1)


def low_grad_kernel(steps, where_ref, *refs):
    if steps:
        half_ref, other_ref, slope_ref, wo_ref, da_ref, out_ref, wo, dh_ref, sems = refs
    else:
        dh_ref, slope_ref, wo_ref, da_ref, wo, sems = refs
    loads = bring(wo_ref, 0, wo, sems, 0, 0)
    if steps:
        place_rows(half_ref, other_ref, where_ref[2], dh_ref)
        out = pltpu.make_async_copy(dh_ref, out_ref, sems.at[len(loads)])
        out.start()
    for cut, copy in loads:
        copy.wait()
        du = lax.dot_general(dh_ref[...], wo[cut, :], NT, preferred_element_type=jnp.float32)
        da_ref[:, cut] = (du * slope_ref[:, cut]).astype(jnp.bfloat16)
    if steps:
        out.wait()


def low_grad(where, dh, w_out, slope, steps):
    rows, hidden = slope.shape
    width = w_out.shape[3]
    outs = [bf16(rows, hidden)] + ([bf16(rows, width)] if steps else [])
    kernel = functools.partial(low_grad_kernel, steps)
    buffers = [(hidden, width)] + ([(rows, width)] if steps else [])
    away = 1 if steps else 0
    return stream(kernel, "low_grad", where, [*dh, slope], [w_out], outs, buffers, len(cuts(hidden)) + 1, away)


def pair_kernel(level, jobs, where_ref, *refs):
    count = len(jobs)
    groups = [refs[6 * i : 6 * i + 6] for i in range(count)]
    outs = refs[-1 - 5 * count : -1 - 4 * count]
    scratch = [refs[-1 - 4 * count :][4 * i : 4 * i + 4] for i in range(count)]
    sems = refs[-1]
    own = []
    for i, (factor, order) in enumerate(jobs):
        a_ref, _, _, b_ref, bn_ref, bf_ref = groups[i]
        right, both, _, raw = scratch[i]
        rows, base = a_ref.shape[0], 8 * i
        own.append(pltpu.make_async_copy(a_ref, both.at[pl.ds(0, rows), :], sems.at[base + 2]))
        own.append(pltpu.make_async_copy(b_ref, right.at[pl.ds(0, rows), :], sems.at[base + 3]))
        if order:
            half = rows // 2
            own.append(pltpu.make_async_copy(bn_ref, raw.at[pl.ds(0, half), :], sems.at[base + 6]))
            own.append(pltpu.make_async_copy(bf_ref, raw.at[pl.ds(half, half), :], sems.at[base + 7]))
    for copy in own:
        copy.start()

    def take(which):
        copies = []
        for i, (factor, order) in enumerate(jobs):
            right, both, _, _ = scratch[i]
            rows, base = groups[i][0].shape[0], 8 * i
            theirs = pl.ds(rows, rows)
            copies.append(pltpu.make_async_copy(groups[i][1 + which], both.at[theirs, :], sems.at[base + 4]))
            if not order:
                copies.append(pltpu.make_async_copy(groups[i][4 + which], right.at[theirs, :], sems.at[base + 5]))
        for copy in copies:
            copy.start()
        for copy in copies:
            copy.wait()

    @pl.when(where_ref[level] == 1)
    def _():
        take(0)

    @pl.when(where_ref[level] != 1)
    def _():
        take(1)

    for copy in own:
        copy.wait()
    last = []
    for i, (factor, order) in enumerate(jobs):
        right, both, slots, raw = scratch[i]
        rows = groups[i][0].shape[0]
        if order:
            pick = places(order, rows, where_ref[3] ^ where_ref[level], where_ref[2])
            right[rows:, :] = jnp.dot(pick, raw[...], preferred_element_type=jnp.float32).astype(jnp.bfloat16)
        copies = []
        for step, cut in enumerate(cuts(both.shape[1], 2 * BLOCK)):
            slot = step % 2
            if step >= 2:
                copies[step - 2].wait()
            value = lax.dot_general(both[:, cut], right[...], TN, preferred_element_type=jnp.float32)
            slots[slot] = (value * factor).astype(jnp.bfloat16)
            copies.append(pltpu.make_async_copy(slots.at[slot], outs[i].at[0, level, cut, :], sems.at[8 * i + slot]))
            copies[-1].start()
        last += copies[-2:]
    for copy in last:
        copy.wait()


def pair_grads(where, level, *jobs):
    operands, befores, outs, scratch, settings = [where], [], [], [], []
    for a, a_mate, b, b_mate, before, order in jobs:
        (rows, left), right = a.shape, b.shape[1]
        operands += [a, *a_mate, b, *b_mate]
        befores += [] if before is None else [before]
        outs.append(bf16(1, 2, left, right))
        scratch += [
            pltpu.VMEM((2 * rows, right), jnp.bfloat16),
            pltpu.VMEM((2 * rows, left), jnp.bfloat16),
            pltpu.VMEM((2, min(2 * BLOCK, left), right), jnp.bfloat16),
            pltpu.VMEM((rows, right), jnp.bfloat16),
        ]
        settings.append((-0.5 / rows**0.5, order))
    return pl.pallas_call(
        functools.partial(pair_kernel, level, settings),
        in_specs=[IN_SMEM] + [ANYWHERE] * (len(operands) + len(befores) - 1),
        out_specs=[ANYWHERE] * len(outs),
        out_shape=outs,
        scratch_shapes=[*scratch, pltpu.SemaphoreType.DMA((8 * len(jobs),))],
        input_output_aliases={len(operands) + i: i for i in range(len(befores))},
        compiler_params=SMALL,
        cost_estimate=FREE,
        name="pair_grads",
    )(*operands, *befores)


def dispatch(spread):
    got = lax.all_to_all(spread, ("path", "shard"), split_axis=0, concat_axis=0, tiled=True)
    return got.reshape(got.shape[0] * got.shape[1], got.shape[2])


def gather_shard(spread):
    got = lax.all_to_all(spread, "shard", split_axis=0, concat_axis=0, tiled=True)
    return got.reshape(got.shape[0] * got.shape[1], got.shape[2])


def scatter_shard(part):
    shards = lax.axis_size("shard")
    blocks = part.reshape(shards, part.shape[0] // shards, part.shape[1])
    return lax.all_to_all(blocks, "shard", split_axis=0, concat_axis=0, tiled=True)


def swap(value, axis, bit):
    return lax.ppermute(value, axis, [(i, i ^ bit) for i in range(lax.axis_size(axis))])


def join(*values):
    return lax.optimization_barrier(jnp.concatenate(values, axis=0))


def gather_steps(own, *others):
    pieces = [swap(own, "shard", bit) for bit in (2, 4, 6)]
    own, *rest = tie(own, *pieces, *others)
    half = join(own, *rest[:3])
    return [half, swap(half, "shard", 1)], rest[3:]


def from_mate(values, *mates):
    paths = lax.axis_size("path")
    mates = mates if len(mates) == len(values) else mates * len(values)
    if paths == 4:
        nears = [swap(v, "path", 1) for v in values]
        sent = [jnp.where(mate == 3, near, v) for near, v, mate in zip(nears, values, mates)]
        return [[near, v] for near, v in zip(nears, sent)]
    me = lax.axis_index("path")
    pairs = []
    for value, mate in zip(values, mates):
        behind = (me - (me ^ mate)) % paths
        mine = value
        for shift in range(1, paths):
            got = lax.ppermute(value, "path", [(i, (i + shift) % paths) for i in range(paths)])
            value, mine = tie(value, jnp.where(behind == shift, got, mine))
        pairs.append([mine, mine])
    return pairs


def along_x(pair):
    if lax.axis_size("path") == 4:
        pair[1] = swap(pair[1], "path", 2)


def body(tokens, routes, cotangent, gains, w_in, w_out, partners):
    paths = lax.axis_size("path")
    shards = lax.axis_size("shard")
    cubes = paths == 4 and shards == 8
    me = lax.axis_index("path")
    shard = lax.axis_index("shard")
    mate_low = partners[0, me] ^ me
    mate_high = partners[1, me] ^ me
    where = jnp.stack([mate_low, mate_high, shard, me])
    none = jnp.int32(0)
    gain = gains[0]
    routes = routes.reshape(-1)

    width, hidden = w_in.shape[2:]

    spread = pack(none, routes, tokens, paths, shards)
    x = dispatch(spread)
    if cubes:
        by_path = pack(me, routes, cotangent, paths, 0)
        rows_1 = join(by_path[0], *[swap(by_path[k], "path", k) for k in (1, 2, 3)])
        hop_1 = swap(rows_1, "shard", 4)
        x, hop_1, where, mate_low, mate_high = tie(x, hop_1, where, mate_low, mate_high)
    n1, u1, slope1, *parts = low_forward(where, x, gain, w_in, w_out, cubes)

    (n1_mate,) = from_mate([n1], mate_low)
    if cubes:
        x_own, keep, give = parts
        rows_2 = join(rows_1, hop_1)
        got, hop_2, n1_mate[1] = tie(swap(give, "shard", 1), swap(rows_2, "shard", 2), n1_mate[1])
        along_x(n1_mate)
        mine, *gives = half_sums(where, keep, got)
        got = [swap(part, "shard", 2 * k + 2) for k, part in enumerate(gives)]
        rows_4 = join(tie(rows_2, mine)[0], hop_2)
        *got, hop_3 = tie(*got, swap(rows_4, "shard", 1))
        h_own = last_sums(x_own, mine, got)
    else:
        along_x(n1_mate)
        h_own, h_spread = settle(where, scatter_shard(parts[0]), x)

    (u1_mate,) = from_mate([u1], mate_low)
    if cubes:
        (half_mate,) = from_mate([rows_4], mate_high)
        dy_own, du2, dy = high_grad(where, join(rows_4, hop_3), w_out, False)
        h, (n1_mate[1], u1_mate[1], half_mate[1]) = gather_steps(h_own, n1_mate[1], u1_mate[1], half_mate[1])
        along_x(u1_mate)
        along_x(half_mate)
        *h, u1_mate[1], du2 = tie(*h, u1_mate[1], du2)
    else:
        h = [gather_shard(h_spread)]
        along_x(u1_mate)
        dy_own, du2, dy = high_grad(where, dispatch(pack(none, routes, cotangent, paths, shards)), w_out, True)
    n2, u2, da2, *parts = high_both(where, h, gain, w_in, du2, cubes)

    da2_mate, u2_mate = from_mate([da2, u2], mate_high)
    if cubes:
        keep, give = parts
        got, da2_mate[1], half_mate[1] = tie(swap(give, "shard", 1), da2_mate[1], half_mate[1])
        along_x(da2_mate)
        mine, *gives = half_sums(where, keep, got)
        got = [swap(part, "shard", 2 * k + 2) for k, part in enumerate(gives)]
        half = jnp.where(mate_high == 1, *half_mate)
        hop_4 = swap(tie(half, mine)[0], "shard", 1)
        *got, hop_4, da2_mate[1], u2_mate[1] = tie(*got, hop_4, da2_mate[1], u2_mate[1])
        along_x(u2_mate)
        dh_own = last_back(dy_own, h_own, gain, mine, got)
    else:
        along_x(da2_mate)
        along_x(u2_mate)
        dh_own, dh_spread = settle_back(where, scatter_shard(parts[0]), dy, h_own, gain)

    (n2_mate,) = from_mate([n2], mate_high)
    if cubes:
        (dh_pair,) = from_mate([dh_own], mate_low)
        along_x(dh_pair)
        dh_piece = jnp.where(mate_low == 1, *dh_pair)
        dh, (u2_mate[1], n2_mate[1], dh_piece) = gather_steps(dh_own, u2_mate[1], n2_mate[1], dh_piece)
        along_x(n2_mate)
        pieces = [swap(dh_piece, "shard", bit) for bit in (4, 2, 6)]
        dy_mate = [half, hop_4]
    else:
        along_x(n2_mate)
        dh = [gather_shard(dh_spread)]
    da1, *dh_ordered = low_grad(where, dh, w_out, slope1, cubes)
    dh = dh_ordered[0] if cubes else dh[0]

    if cubes:
        da1, n2_mate[1], *pieces = tie(da1, n2_mate[1], *pieces)
    (da1_mate,) = from_mate([da1], mate_low)
    along_x(da1_mate)
    if cubes:
        dh_half = join(dh_piece, *pieces)
        dh_mate = [dh_half, swap(dh_half, "shard", 1)]
    else:
        (dh_mate,) = from_mate([dh], mate_low)
        along_x(dh_mate)
        (dy_mate,) = from_mate([dy], mate_high)
        along_x(dy_mate)
    delta_in, delta_out = pair_grads(
        where,
        1,
        (n2, n2_mate, da2, da2_mate, None, ""),
        (u2, u2_mate, dy, dy_mate, None, "dispatch" if cubes else ""),
    )
    delta_in, delta_out = pair_grads(
        where,
        0,
        (n1, n1_mate, da1, da1_mate, delta_in, ""),
        (u1, u1_mate, dh, dh_mate, delta_out, "gather" if cubes else ""),
    )
    return (delta_in, delta_out)


def solution(mesh):
    in_specs = (
        P(("path", "shard"), None),
        P(("path", "shard"), None),
        P(("path", "shard"), None),
        P("path", None, None),
        P("path", None, None, "shard"),
        P("path", None, "shard", None),
        P(),
    )
    out_specs = (P("path", None, None, "shard"), P("path", None, "shard", None))
    return jax.shard_map(body, mesh=mesh, in_specs=in_specs, out_specs=out_specs, check_vma=False)
```

```python
import functools

import jax
import jax.numpy as jnp
from jax import lax
from jax.experimental import pallas as pl
from jax.experimental.pallas import tpu as pltpu
from jax.sharding import PartitionSpec as P

SLOTS = 16
BLOCK = 256
ROOT = 0.7978845608028654
CUBE = 0.044715
NT = (((1,), (1,)), ((), ()))
TN = (((0,), (0,)), ((), ()))
PARAMS = pltpu.CompilerParams(vmem_limit_bytes=16 * 1024 * 1024)
SMALL = pltpu.CompilerParams(vmem_limit_bytes=56 * 1024 * 1024)
STREAM = pltpu.CompilerParams(vmem_limit_bytes=50 * 1024 * 1024)
IN_VMEM = pl.BlockSpec(memory_space=pltpu.VMEM)
IN_SMEM = pl.BlockSpec(memory_space=pltpu.SMEM)
ANYWHERE = pl.BlockSpec(memory_space=pl.ANY)
FREE = pl.CostEstimate(flops=0, bytes_accessed=0, transcendentals=0)


def bf16(*shape):
    return jax.ShapeDtypeStruct(shape, jnp.bfloat16)


def f32(*shape):
    return jax.ShapeDtypeStruct(shape, jnp.float32)


def cuts(size, step=BLOCK):
    step = min(step, size)
    return [pl.ds(start, step) for start in range(0, size, step)]


def tie(*values):
    return lax.optimization_barrier(values)


def call(kernel, name, where, arrays, outs):
    operands = [] if where is None else [where]
    return pl.pallas_call(
        kernel,
        in_specs=[IN_SMEM] * len(operands) + [IN_VMEM] * len(arrays),
        out_specs=[IN_VMEM] * len(outs),
        out_shape=outs,
        compiler_params=PARAMS,
        cost_estimate=FREE,
        name=name,
    )(*operands, *arrays)


def stream(kernel, name, where, arrays, weights, outs, buffers, copies):
    operands = [] if where is None else [where]
    return pl.pallas_call(
        kernel,
        in_specs=[IN_SMEM] * len(operands) + [IN_VMEM] * len(arrays) + [ANYWHERE] * len(weights),
        out_specs=[IN_VMEM] * len(outs),
        out_shape=outs,
        scratch_shapes=[pltpu.VMEM(shape, jnp.bfloat16) for shape in buffers] + [pltpu.SemaphoreType.DMA((copies,))],
        compiler_params=STREAM,
        cost_estimate=FREE,
        name=name,
    )(*operands, *arrays, *weights)


def bring(w_ref, level, buffer, sems, first, along):
    pieces = []
    for i, cut in enumerate(cuts(buffer.shape[along])):
        source = w_ref.at[0, level, cut, :] if along == 0 else w_ref.at[0, level, :, cut]
        target = buffer.at[cut, :] if along == 0 else buffer.at[:, cut]
        copy = pltpu.make_async_copy(source, target, sems.at[first + i])
        copy.start()
        pieces.append((cut, copy))
    return pieces


def norm_value(v, gain):
    return v * lax.rsqrt(jnp.mean(v * v, axis=-1, keepdims=True) + 1e-05) * gain.astype(jnp.float32)


def gelu_both(a):
    t = jnp.tanh(ROOT * (a + CUBE * (a * a * a)))
    half = 0.5 * (1.0 + t)
    slope = half + 0.5 * a * (1.0 - t * t) * (ROOT * (1.0 + (3.0 * CUBE) * (a * a)))
    return a * half, slope


def slots_of_rows(routes_ref, cap, flip):
    count = routes_ref.shape[0]
    down = lax.broadcasted_iota(jnp.int32, (count, count), 0)
    along = lax.broadcasted_iota(jnp.int32, (count, count), 1)
    route_down = jnp.zeros((count, count), jnp.int32)
    route_along = jnp.zeros((count, count), jnp.int32)
    for r in range(count):
        route = routes_ref[r]
        route_down = jnp.where(down == r, route, route_down)
        route_along = jnp.where(along == r, route, route_along)
    earlier = jnp.where((route_down == route_along) & (down < along), 1, 0)
    rank = jnp.sum(earlier, axis=0, keepdims=True)
    return (route_along[0:1, :] ^ flip) * cap + rank


def pack_kernel(copies, flip_ref, routes_ref, rows_ref, *out_refs):
    count = routes_ref.shape[0]
    cap = out_refs[0].shape[-2]
    slots = slots_of_rows(routes_ref, cap, flip_ref[0])
    for group in range(SLOTS // cap):
        want = group * cap + lax.broadcasted_iota(jnp.int32, (cap, count), 0)
        pick = (want == slots).astype(jnp.float32).astype(jnp.bfloat16)
        value = jnp.dot(pick, rows_ref[...], preferred_element_type=jnp.float32).astype(jnp.bfloat16)
        if copies == 0:
            out_refs[group][...] = value
        for copy in range(copies):
            out_refs[0][group * copies + copy] = value


def pack(flip, routes, rows, paths, copies):
    cap, width = SLOTS // paths, rows.shape[1]
    outs = [bf16(paths * copies, cap, width)] if copies else [bf16(cap, width)] * paths
    got = pl.pallas_call(
        functools.partial(pack_kernel, copies),
        in_specs=[IN_SMEM, IN_SMEM, IN_VMEM],
        out_specs=[IN_VMEM] * len(outs),
        out_shape=outs,
        compiler_params=SMALL,
        cost_estimate=FREE,
        name="pack",
    )(flip.reshape(1), routes, rows)
    return got[0] if copies else got


def settle_kernel(where_ref, got_ref, x_ref, own_ref, spread_ref):
    count, rows, _ = got_ref.shape
    total = x_ref[pl.ds(pl.multiple_of(where_ref[2] * rows, rows), rows), :].astype(jnp.float32)
    for i in range(count):
        total += got_ref[i].astype(jnp.float32)
    total = total.astype(jnp.bfloat16)
    own_ref[...] = total
    for i in range(count):
        spread_ref[i] = total


def settle(where, got, x):
    count, rows, width = got.shape
    return call(settle_kernel, "settle", where, [got, x], [bf16(rows, width), bf16(count, rows, width)])


def pull_back(dy, h, gain, grad):
    grad = grad * gain.astype(jnp.float32)
    h = h.astype(jnp.float32)
    scale = lax.rsqrt(jnp.mean(h * h, axis=-1, keepdims=True) + 1e-05)
    unit = h * scale
    pull = scale * (grad - unit * jnp.mean(grad * unit, axis=-1, keepdims=True))
    return (dy.astype(jnp.float32) + pull).astype(jnp.bfloat16)


def settle_back_kernel(where_ref, got_ref, dy_ref, h_ref, gain_ref, own_ref, spread_ref):
    count, rows, _ = got_ref.shape
    grad = got_ref[0].astype(jnp.float32)
    for i in range(1, count):
        grad += got_ref[i].astype(jnp.float32)
    dy = dy_ref[pl.ds(pl.multiple_of(where_ref[2] * rows, rows), rows), :]
    total = pull_back(dy, h_ref[...], gain_ref[1:2, :], grad)
    own_ref[...] = total
    for i in range(count):
        spread_ref[i] = total


def settle_back(where, got, dy, h_own, gains):
    count, rows, width = got.shape
    outs = [bf16(rows, width), bf16(count, rows, width)]
    return call(settle_back_kernel, "settle_back", where, [got, dy, h_own, gains], outs)


def half_kernel(where_ref, keep_ref, got_ref, mine_ref, *rest):
    gives, total = rest[:-1], rest[-1]
    total[...] = keep_ref[...].astype(jnp.float32) + got_ref[...].astype(jnp.float32)
    z = where_ref[2] >> 1
    mine_ref[...] = total[z]
    for step, give_ref in enumerate(gives):
        give_ref[...] = total[z ^ (step + 1)].astype(jnp.bfloat16)


def half_sums(where, keep, got):
    groups, rows, width = keep.shape
    return pl.pallas_call(
        half_kernel,
        in_specs=[IN_SMEM] + [IN_VMEM] * 2,
        out_specs=[IN_VMEM] * groups,
        out_shape=[f32(rows, width)] + [bf16(rows, width)] * (groups - 1),
        scratch_shapes=[pltpu.VMEM(keep.shape, jnp.float32)],
        compiler_params=PARAMS,
        cost_estimate=FREE,
        name="half_sums",
    )(where, keep, got)


def last_kernel(x_ref, mine_ref, *rest):
    total = x_ref[...].astype(jnp.float32) + mine_ref[...]
    for got_ref in rest[:-1]:
        total += got_ref[...].astype(jnp.float32)
    rest[-1][...] = total.astype(jnp.bfloat16)


def last_sums(x_own, mine, got):
    return call(last_kernel, "last_sums", None, [x_own, mine, *got], [bf16(*x_own.shape)])[0]


def last_back_kernel(dy_ref, h_ref, gain_ref, mine_ref, *rest):
    grad = mine_ref[...]
    for got_ref in rest[:-1]:
        grad += got_ref[...].astype(jnp.float32)
    rest[-1][...] = pull_back(dy_ref[...], h_ref[...], gain_ref[1:2, :], grad)


def last_back(dy_own, h_own, gains, mine, got):
    return call(last_back_kernel, "last_back", None, [dy_own, h_own, gains, mine, *got], [bf16(*h_own.shape)])[0]


def low_kernel(steps, where_ref, x_ref, gain_ref, wi_ref, wo_ref, n_ref, u_ref, slope_ref, *rest):
    if steps:
        own_ref, keep_ref, give_ref, wi, wo, part_ref, sems = rest
        own_ref[...] = x_ref[pl.ds(pl.multiple_of(where_ref[2] * SLOTS, SLOTS), SLOTS), :]
    else:
        part_ref, wi, wo, sems = rest
    into = bring(wi_ref, 0, wi, sems, 0, 1)
    n_ref[...] = norm_value(x_ref[...].astype(jnp.float32), gain_ref[0:1, :]).astype(jnp.bfloat16)
    for i, (cut, copy) in enumerate(into):
        copy.wait()
        if i == 0:
            out_of = bring(wo_ref, 0, wo, sems, len(into), 1)
        a = jnp.dot(n_ref[...], wi[:, cut], preferred_element_type=jnp.float32)
        u, slope = gelu_both(a)
        u_ref[:, cut] = u.astype(jnp.bfloat16)
        slope_ref[:, cut] = slope
    for cut, copy in out_of:
        copy.wait()
        part = jnp.dot(u_ref[...], wo[:, cut], preferred_element_type=jnp.float32)
        part_ref[:, cut] = part.astype(jnp.bfloat16)
    if steps:
        split_rows(part_ref, where_ref[2], keep_ref, give_ref)


def split_rows(part_ref, shard, keep_ref, give_ref):
    groups = part_ref.shape[0] // (2 * SLOTS)
    for y in range(2):

        @pl.when((shard & 1) == y)
        def _():
            for z in range(groups):
                start = z * 2 * SLOTS
                keep_ref[z] = part_ref[start + y * SLOTS : start + (y + 1) * SLOTS, :]
                give_ref[z] = part_ref[start + (1 - y) * SLOTS : start + (2 - y) * SLOTS, :]


def place_rows(half_ref, other_ref, shard, out_ref):
    for step in range(half_ref.shape[0] // SLOTS):
        for flip, source in enumerate((half_ref, other_ref)):
            start = pl.multiple_of((shard ^ (2 * step) ^ flip) * SLOTS, SLOTS)
            out_ref[pl.ds(start, SLOTS), :] = source[step * SLOTS : (step + 1) * SLOTS, :]


def low_forward(where, x, gains, w_in, w_out, steps):
    rows, width = x.shape
    hidden = w_in.shape[3]
    outs = [bf16(rows, width), bf16(rows, hidden), f32(rows, hidden)]
    buffers = [(width, hidden), (hidden, width)]
    if steps:
        outs += [bf16(SLOTS, width)] + [bf16(rows // (2 * SLOTS), SLOTS, width)] * 2
        buffers.append((rows, width))
    else:
        outs.append(bf16(rows, width))
    copies = len(cuts(hidden)) + len(cuts(width))
    return stream(functools.partial(low_kernel, steps), "low_forward", where, [x, gains], [w_in, w_out], outs, buffers, copies)


def high_kernel(steps, where_ref, *refs):
    if steps:
        half_ref, other_ref, gain_ref, du_ref, wi_ref, n_ref, u_ref, da_ref, keep_ref, give_ref, wi, h_ref, part_ref, sems = refs
    else:
        h_ref, gain_ref, du_ref, wi_ref, n_ref, u_ref, da_ref, part_ref, wi, sems = refs
    into = bring(wi_ref, 1, wi, sems, 0, 1)
    if steps:
        place_rows(half_ref, other_ref, where_ref[2], h_ref)
    n_ref[...] = norm_value(h_ref[...].astype(jnp.float32), gain_ref[1:2, :]).astype(jnp.bfloat16)
    for cut, copy in into:
        copy.wait()
        a = jnp.dot(n_ref[...], wi[:, cut], preferred_element_type=jnp.float32)
        u, slope = gelu_both(a)
        u_ref[:, cut] = u.astype(jnp.bfloat16)
        da_ref[:, cut] = (slope * du_ref[:, cut]).astype(jnp.bfloat16)
    for cut in cuts(wi.shape[0]):
        part = lax.dot_general(da_ref[...], wi[cut, :], NT, preferred_element_type=jnp.float32)
        part_ref[:, cut] = part.astype(jnp.bfloat16)
    if steps:
        split_rows(part_ref, where_ref[2], keep_ref, give_ref)


def high_both(where, h, gains, w_in, du, steps):
    rows, width = du.shape[0], gains.shape[1]
    hidden = w_in.shape[3]
    outs = [bf16(rows, width), bf16(rows, hidden), bf16(rows, hidden)]
    buffers = [(width, hidden)]
    if steps:
        outs += [bf16(rows // (2 * SLOTS), SLOTS, width)] * 2
        buffers += [(rows, width)] * 2
    else:
        outs.append(bf16(rows, width))
    kernel = functools.partial(high_kernel, steps)
    return stream(kernel, "high_both", where, [*h, gains, du], [w_in], outs, buffers, len(cuts(hidden)))


def places(order, rows, path, shard):
    to = lax.broadcasted_iota(jnp.int32, (rows, rows), 0)
    source = lax.broadcasted_iota(jnp.int32, (rows, rows), 1)
    if order == "dispatch":
        far = ((to >> 2) & 7) ^ shard
        block = ((far & 1) << 2) | (far & 2) | (far >> 2)
        wanted = block * 16 + ((to >> 5) ^ path) * 4 + (to & 3)
    else:
        far = (to >> 4) ^ shard
        block = ((far & 1) << 2) | (far >> 1)
        wanted = block * 16 + (to & 15)
    return (source == wanted).astype(jnp.float32).astype(jnp.bfloat16)


def high_grad_kernel(ordered, where_ref, raw_ref, wo_ref, own_ref, du_ref, dy_ref, wo, sems):
    pieces = bring(wo_ref, 1, wo, sems, 0, 0)
    if ordered:
        dy_ref[...] = raw_ref[...]
    else:
        pick = places("dispatch", raw_ref.shape[0], where_ref[3], where_ref[2])
        dy_ref[...] = jnp.dot(pick, raw_ref[...], preferred_element_type=jnp.float32).astype(jnp.bfloat16)
    own_ref[...] = dy_ref[pl.ds(pl.multiple_of(where_ref[2] * SLOTS, SLOTS), SLOTS), :]
    for cut, copy in pieces:
        copy.wait()
        du_ref[:, cut] = lax.dot_general(dy_ref[...], wo[cut, :], NT, preferred_element_type=jnp.float32)


def high_grad(where, raw, w_out, ordered):
    rows, width = raw.shape
    hidden = w_out.shape[2]
    outs = [bf16(SLOTS, width), f32(rows, hidden), bf16(rows, width)]
    kernel = functools.partial(high_grad_kernel, ordered)
    return stream(kernel, "high_grad", where, [raw], [w_out], outs, [(hidden, width)], len(cuts(hidden)))


def low_grad_kernel(steps, where_ref, *refs):
    if steps:
        half_ref, other_ref, slope_ref, wo_ref, da_ref, wo, dh_ref, sems = refs
    else:
        dh_ref, slope_ref, wo_ref, da_ref, wo, sems = refs
    loads = bring(wo_ref, 0, wo, sems, 0, 0)
    if steps:
        place_rows(half_ref, other_ref, where_ref[2], dh_ref)
    for cut, copy in loads:
        copy.wait()
        du = lax.dot_general(dh_ref[...], wo[cut, :], NT, preferred_element_type=jnp.float32)
        da_ref[:, cut] = (du * slope_ref[:, cut]).astype(jnp.bfloat16)


def low_grad(where, dh, w_out, slope, steps):
    rows, hidden = slope.shape
    width = w_out.shape[3]
    outs = [bf16(rows, hidden)]
    kernel = functools.partial(low_grad_kernel, steps)
    buffers = [(hidden, width)] + ([(rows, width)] if steps else [])
    return stream(kernel, "low_grad", where, [*dh, slope], [w_out], outs, buffers, len(cuts(hidden)))[0]


def pair_kernel(level, jobs, where_ref, *refs):
    count = len(jobs)
    groups, used = [], 0
    for _, _, halves in jobs:
        size = 5 + halves
        groups.append(refs[used : used + size])
        used += size
    outs = refs[-1 - 5 * count : -1 - 4 * count]
    scratch = [refs[-1 - 4 * count :][4 * i : 4 * i + 4] for i in range(count)]
    sems = refs[-1]

    def run(which):
        waits = []
        for i, (factor, order, halves) in enumerate(jobs):
            a_ref, *b_refs = groups[i][0], *groups[i][3:]
            right, both, _, raw = scratch[i]
            rows, base = a_ref.shape[0], 8 * i
            half, mine, theirs = rows // 2, pl.ds(0, rows), pl.ds(rows, rows)
            copies = [
                pltpu.make_async_copy(a_ref, both.at[mine, :], sems.at[base + 2]),
                pltpu.make_async_copy(groups[i][1 + which], both.at[theirs, :], sems.at[base + 3]),
            ]
            targets = [raw.at[pl.ds(place * half, half), :] for place in range(4)] if order else []
            if halves == 1:
                copies.append(pltpu.make_async_copy(b_refs[0], right.at[mine, :], sems.at[base + 4]))
            else:
                copies.append(pltpu.make_async_copy(b_refs[0], targets[0], sems.at[base + 4]))
                copies.append(pltpu.make_async_copy(b_refs[1], targets[1], sems.at[base + 5]))
            if order:
                copies.append(pltpu.make_async_copy(b_refs[-2], targets[2], sems.at[base + 6]))
                copies.append(pltpu.make_async_copy(b_refs[-1], targets[3], sems.at[base + 7]))
            else:
                copies.append(pltpu.make_async_copy(b_refs[1 + which], right.at[theirs, :], sems.at[base + 6]))
            for copy in copies:
                copy.start()
            waits.append(copies)
        last = []
        for i, (factor, order, halves) in enumerate(jobs):
            right, both, slots, raw = scratch[i]
            rows = groups[i][0].shape[0]
            for copy in waits[i]:
                copy.wait()
            if order:
                for part in (0, 1) if halves == 2 else (1,):
                    path = where_ref[3] ^ where_ref[level] if part else where_ref[3]
                    pick, span = places(order, rows, path, where_ref[2]), pl.ds(part * rows, rows)
                    value = jnp.dot(pick, raw[span, :], preferred_element_type=jnp.float32)
                    right[span, :] = value.astype(jnp.bfloat16)
            copies = []
            for step, cut in enumerate(cuts(both.shape[1], 2 * BLOCK)):
                slot = step % 2
                if step >= 2:
                    copies[step - 2].wait()
                value = lax.dot_general(both[:, cut], right[...], TN, preferred_element_type=jnp.float32)
                slots[slot] = (value * factor).astype(jnp.bfloat16)
                target = outs[i].at[0, level, cut, :]
                copies.append(pltpu.make_async_copy(slots.at[slot], target, sems.at[8 * i + slot]))
                copies[-1].start()
            last += copies[-2:]
        for copy in last:
            copy.wait()

    @pl.when(where_ref[level] == 1)
    def _():
        run(0)

    @pl.when(where_ref[level] != 1)
    def _():
        run(1)


def pair_grads(where, level, *jobs):
    operands, befores, outs, scratch, settings = [where], [], [], [], []
    for a, a_mate, b, b_mate, before, order in jobs:
        (rows, left), right = a.shape, b[0].shape[1]
        operands += [a, *a_mate, *b, *b_mate]
        befores += [] if before is None else [before]
        outs.append(bf16(1, 2, left, right))
        scratch += [
            pltpu.VMEM((2 * rows, right), jnp.bfloat16),
            pltpu.VMEM((2 * rows, left), jnp.bfloat16),
            pltpu.VMEM((2, min(2 * BLOCK, left), right), jnp.bfloat16),
            pltpu.VMEM((2 * rows if order else SLOTS, right), jnp.bfloat16),
        ]
        settings.append((-0.5 / rows**0.5, order, len(b)))
    return pl.pallas_call(
        functools.partial(pair_kernel, level, settings),
        in_specs=[IN_SMEM] + [ANYWHERE] * (len(operands) + len(befores) - 1),
        out_specs=[ANYWHERE] * len(outs),
        out_shape=outs,
        scratch_shapes=[*scratch, pltpu.SemaphoreType.DMA((8 * len(jobs),))],
        input_output_aliases={len(operands) + i: i for i in range(len(befores))},
        compiler_params=SMALL,
        cost_estimate=FREE,
        name="pair_grads",
    )(*operands, *befores)


def dispatch(spread):
    got = lax.all_to_all(spread, ("path", "shard"), split_axis=0, concat_axis=0, tiled=True)
    return got.reshape(got.shape[0] * got.shape[1], got.shape[2])


def gather_shard(spread):
    got = lax.all_to_all(spread, "shard", split_axis=0, concat_axis=0, tiled=True)
    return got.reshape(got.shape[0] * got.shape[1], got.shape[2])


def scatter_shard(part):
    shards = lax.axis_size("shard")
    blocks = part.reshape(shards, part.shape[0] // shards, part.shape[1])
    return lax.all_to_all(blocks, "shard", split_axis=0, concat_axis=0, tiled=True)


def swap(value, axis, bit):
    return lax.ppermute(value, axis, [(i, i ^ bit) for i in range(lax.axis_size(axis))])


def join(*values):
    return lax.optimization_barrier(jnp.concatenate(values, axis=0))


def gather_steps(own, *others):
    pieces = [swap(own, "shard", bit) for bit in (2, 4, 6)]
    own, *rest = tie(own, *pieces, *others)
    half = join(own, *rest[:3])
    return [half, swap(half, "shard", 1)], rest[3:]


def from_mate(values, *mates):
    paths = lax.axis_size("path")
    mates = mates if len(mates) == len(values) else mates * len(values)
    if paths == 4:
        nears = [swap(v, "path", 1) for v in values]
        sent = [jnp.where(mate == 3, near, v) for near, v, mate in zip(nears, values, mates)]
        return [[near, v] for near, v in zip(nears, sent)]
    me = lax.axis_index("path")
    pairs = []
    for value, mate in zip(values, mates):
        behind = (me - (me ^ mate)) % paths
        mine = value
        for shift in range(1, paths):
            got = lax.ppermute(value, "path", [(i, (i + shift) % paths) for i in range(paths)])
            value, mine = tie(value, jnp.where(behind == shift, got, mine))
        pairs.append([mine, mine])
    return pairs


def along_x(pair):
    if lax.axis_size("path") == 4:
        pair[1] = swap(pair[1], "path", 2)


def body(tokens, routes, cotangent, gains, w_in, w_out, partners):
    paths = lax.axis_size("path")
    shards = lax.axis_size("shard")
    cubes = paths == 4 and shards == 8
    me = lax.axis_index("path")
    shard = lax.axis_index("shard")
    mate_low = partners[0, me] ^ me
    mate_high = partners[1, me] ^ me
    where = jnp.stack([mate_low, mate_high, shard, me])
    none = jnp.int32(0)
    gain = gains[0]
    routes = routes.reshape(-1)

    width, hidden = w_in.shape[2:]

    spread = pack(none, routes, tokens, paths, shards)
    x = dispatch(spread)
    if cubes:
        by_path = pack(me, routes, cotangent, paths, 0)
        rows_1 = join(by_path[0], *[swap(by_path[k], "path", k) for k in (1, 2, 3)])
        hop_1 = swap(rows_1, "shard", 4)
        x, hop_1, where, mate_low, mate_high = tie(x, hop_1, where, mate_low, mate_high)
    n1, u1, slope1, *parts = low_forward(where, x, gain, w_in, w_out, cubes)

    (n1_mate,) = from_mate([n1], mate_low)
    if cubes:
        x_own, keep, give = parts
        rows_2 = join(rows_1, hop_1)
        got, hop_2, n1_mate[1] = tie(swap(give, "shard", 1), swap(rows_2, "shard", 2), n1_mate[1])
        along_x(n1_mate)
        mine, *gives = half_sums(where, keep, got)
        got = [swap(part, "shard", 2 * k + 2) for k, part in enumerate(gives)]
        rows_4 = join(tie(rows_2, mine)[0], hop_2)
        *got, hop_3 = tie(*got, swap(rows_4, "shard", 1))
        h_own = last_sums(x_own, mine, got)
    else:
        along_x(n1_mate)
        h_own, h_spread = settle(where, scatter_shard(parts[0]), x)

    (u1_mate,) = from_mate([u1], mate_low)
    if cubes:
        (half_mate,) = from_mate([rows_4], mate_high)
        dy_own, du2, dy = high_grad(where, join(rows_4, hop_3), w_out, False)
        h, (n1_mate[1], u1_mate[1], half_mate[1]) = gather_steps(h_own, n1_mate[1], u1_mate[1], half_mate[1])
        along_x(u1_mate)
        along_x(half_mate)
        *h, u1_mate[1], du2 = tie(*h, u1_mate[1], du2)
    else:
        h = [gather_shard(h_spread)]
        along_x(u1_mate)
        dy = dispatch(pack(none, routes, cotangent, paths, shards))
        dy_own, du2, dy = high_grad(where, dy, w_out, True)
    n2, u2, da2, *parts = high_both(where, h, gain, w_in, du2, cubes)

    da2_mate, u2_mate = from_mate([da2, u2], mate_high)
    if cubes:
        keep, give = parts
        got, da2_mate[1], half_mate[1] = tie(swap(give, "shard", 1), da2_mate[1], half_mate[1])
        along_x(da2_mate)
        mine, *gives = half_sums(where, keep, got)
        got = [swap(part, "shard", 2 * k + 2) for k, part in enumerate(gives)]
        half = jnp.where(mate_high == 1, *half_mate)
        hop_4 = swap(tie(half, mine)[0], "shard", 1)
        *got, hop_4, da2_mate[1], u2_mate[1] = tie(*got, hop_4, da2_mate[1], u2_mate[1])
        along_x(u2_mate)
        dh_own = last_back(dy_own, h_own, gain, mine, got)
    else:
        along_x(da2_mate)
        along_x(u2_mate)
        dh_own, dh_spread = settle_back(where, scatter_shard(parts[0]), dy, h_own, gain)

    (n2_mate,) = from_mate([n2], mate_high)
    if cubes:
        (dh_pair,) = from_mate([dh_own], mate_low)
        dh_own, dh_pair[1] = tie(dh_own, dh_pair[1])
        along_x(dh_pair)
        dh_piece = jnp.where(mate_low == 1, *dh_pair)
        dh, (u2_mate[1], n2_mate[1], dh_piece) = gather_steps(dh_own, u2_mate[1], n2_mate[1], dh_piece)
        along_x(n2_mate)
        pieces = [swap(dh_piece, "shard", bit) for bit in (2, 4, 6)]
        dy_mate = [half, hop_4]
    else:
        along_x(n2_mate)
        dh = [gather_shard(dh_spread)]
    da1 = low_grad(where, dh, w_out, slope1, cubes)

    if cubes:
        da1, n2_mate[1], *pieces = tie(da1, n2_mate[1], *pieces)
    (da1_mate,) = from_mate([da1], mate_low)
    along_x(da1_mate)
    if cubes:
        dh_half = join(dh_piece, *pieces)
        dh_mate = [dh_half, swap(dh_half, "shard", 1)]
    else:
        (dh_mate,) = from_mate(dh, mate_low)
        along_x(dh_mate)
        (dy_mate,) = from_mate([dy], mate_high)
        along_x(dy_mate)
    delta_in, delta_out = pair_grads(
        where,
        1,
        (n2, n2_mate, [da2], da2_mate, None, ""),
        (u2, u2_mate, [dy], dy_mate, None, "dispatch" if cubes else ""),
    )
    delta_in, delta_out = pair_grads(
        where,
        0,
        (n1, n1_mate, [da1], da1_mate, delta_in, ""),
        (u1, u1_mate, dh, dh_mate, delta_out, "gather" if cubes else ""),
    )
    return (delta_in, delta_out)


def solution(mesh):
    in_specs = (
        P(("path", "shard"), None),
        P(("path", "shard"), None),
        P(("path", "shard"), None),
        P("path", None, None),
        P("path", None, None, "shard"),
        P("path", None, "shard", None),
        P(),
    )
    out_specs = (P("path", None, None, "shard"), P("path", None, "shard", None))
    return jax.shard_map(body, mesh=mesh, in_specs=in_specs, out_specs=out_specs, check_vma=False)
```

```python
import functools

import jax
import jax.numpy as jnp
from jax import lax
from jax.experimental import pallas as pl
from jax.experimental.pallas import tpu as pltpu
from jax.sharding import PartitionSpec as P

SLOTS = 16
BLOCK = 256
ROOT = 0.7978845608028654
CUBE = 0.044715
NT = (((1,), (1,)), ((), ()))
TN = (((0,), (0,)), ((), ()))
PARAMS = pltpu.CompilerParams(vmem_limit_bytes=16 * 1024 * 1024)
SMALL = pltpu.CompilerParams(vmem_limit_bytes=56 * 1024 * 1024)
STREAM = pltpu.CompilerParams(vmem_limit_bytes=50 * 1024 * 1024)
IN_VMEM = pl.BlockSpec(memory_space=pltpu.VMEM)
IN_SMEM = pl.BlockSpec(memory_space=pltpu.SMEM)
ANYWHERE = pl.BlockSpec(memory_space=pl.ANY)
FREE = pl.CostEstimate(flops=0, bytes_accessed=0, transcendentals=0)


def bf16(*shape):
    return jax.ShapeDtypeStruct(shape, jnp.bfloat16)


def f32(*shape):
    return jax.ShapeDtypeStruct(shape, jnp.float32)


def cuts(size, step=BLOCK):
    step = min(step, size)
    return [pl.ds(start, step) for start in range(0, size, step)]


def tie(*values):
    return lax.optimization_barrier(values)


def call(kernel, name, where, arrays, outs):
    operands = [] if where is None else [where]
    return pl.pallas_call(
        kernel,
        in_specs=[IN_SMEM] * len(operands) + [IN_VMEM] * len(arrays),
        out_specs=[IN_VMEM] * len(outs),
        out_shape=outs,
        compiler_params=PARAMS,
        cost_estimate=FREE,
        name=name,
    )(*operands, *arrays)


def stream(kernel, name, where, arrays, weights, outs, buffers, copies):
    operands = [] if where is None else [where]
    return pl.pallas_call(
        kernel,
        in_specs=[IN_SMEM] * len(operands) + [IN_VMEM] * len(arrays) + [ANYWHERE] * len(weights),
        out_specs=[IN_VMEM] * len(outs),
        out_shape=outs,
        scratch_shapes=[pltpu.VMEM(shape, jnp.bfloat16) for shape in buffers] + [pltpu.SemaphoreType.DMA((copies,))],
        compiler_params=STREAM,
        cost_estimate=FREE,
        name=name,
    )(*operands, *arrays, *weights)


def bring(w_ref, level, buffer, sems, first, along):
    pieces = []
    for i, cut in enumerate(cuts(buffer.shape[along])):
        source = w_ref.at[0, level, cut, :] if along == 0 else w_ref.at[0, level, :, cut]
        target = buffer.at[cut, :] if along == 0 else buffer.at[:, cut]
        copy = pltpu.make_async_copy(source, target, sems.at[first + i])
        copy.start()
        pieces.append((cut, copy))
    return pieces


def norm_value(v, gain):
    return v * lax.rsqrt(jnp.mean(v * v, axis=-1, keepdims=True) + 1e-05) * gain.astype(jnp.float32)


def gelu_both(a):
    t = jnp.tanh(ROOT * (a + CUBE * (a * a * a)))
    half = 0.5 * (1.0 + t)
    slope = half + 0.5 * a * (1.0 - t * t) * (ROOT * (1.0 + (3.0 * CUBE) * (a * a)))
    return a * half, slope


def slots_of_rows(routes_ref, cap, flip):
    count = routes_ref.shape[0]
    down = lax.broadcasted_iota(jnp.int32, (count, count), 0)
    along = lax.broadcasted_iota(jnp.int32, (count, count), 1)
    route_down = jnp.zeros((count, count), jnp.int32)
    route_along = jnp.zeros((count, count), jnp.int32)
    for r in range(count):
        route = routes_ref[r]
        route_down = jnp.where(down == r, route, route_down)
        route_along = jnp.where(along == r, route, route_along)
    earlier = jnp.where((route_down == route_along) & (down < along), 1, 0)
    rank = jnp.sum(earlier, axis=0, keepdims=True)
    return (route_along[0:1, :] ^ flip) * cap + rank


def pack_kernel(copies, flip_ref, routes_ref, rows_ref, *out_refs):
    count = routes_ref.shape[0]
    cap = out_refs[0].shape[-2]
    slots = slots_of_rows(routes_ref, cap, flip_ref[0])
    for group in range(SLOTS // cap):
        want = group * cap + lax.broadcasted_iota(jnp.int32, (cap, count), 0)
        pick = (want == slots).astype(jnp.float32).astype(jnp.bfloat16)
        value = jnp.dot(pick, rows_ref[...], preferred_element_type=jnp.float32).astype(jnp.bfloat16)
        if copies == 0:
            out_refs[group][...] = value
        for copy in range(copies):
            out_refs[0][group * copies + copy] = value


def pack(flip, routes, rows, paths, copies):
    cap, width = SLOTS // paths, rows.shape[1]
    outs = [bf16(paths * copies, cap, width)] if copies else [bf16(cap, width)] * paths
    got = pl.pallas_call(
        functools.partial(pack_kernel, copies),
        in_specs=[IN_SMEM, IN_SMEM, IN_VMEM],
        out_specs=[IN_VMEM] * len(outs),
        out_shape=outs,
        compiler_params=SMALL,
        cost_estimate=FREE,
        name="pack",
    )(flip.reshape(1), routes, rows)
    return got[0] if copies else got


def settle_kernel(where_ref, got_ref, x_ref, own_ref, spread_ref):
    count, rows, _ = got_ref.shape
    total = x_ref[pl.ds(pl.multiple_of(where_ref[2] * rows, rows), rows), :].astype(jnp.float32)
    for i in range(count):
        total += got_ref[i].astype(jnp.float32)
    total = total.astype(jnp.bfloat16)
    own_ref[...] = total
    for i in range(count):
        spread_ref[i] = total


def settle(where, got, x):
    count, rows, width = got.shape
    return call(settle_kernel, "settle", where, [got, x], [bf16(rows, width), bf16(count, rows, width)])


def pull_back(dy, h, gain, grad):
    grad = grad * gain.astype(jnp.float32)
    h = h.astype(jnp.float32)
    scale = lax.rsqrt(jnp.mean(h * h, axis=-1, keepdims=True) + 1e-05)
    unit = h * scale
    pull = scale * (grad - unit * jnp.mean(grad * unit, axis=-1, keepdims=True))
    return (dy.astype(jnp.float32) + pull).astype(jnp.bfloat16)


def settle_back_kernel(where_ref, got_ref, dy_ref, h_ref, gain_ref, own_ref, spread_ref):
    count, rows, _ = got_ref.shape
    grad = got_ref[0].astype(jnp.float32)
    for i in range(1, count):
        grad += got_ref[i].astype(jnp.float32)
    dy = dy_ref[pl.ds(pl.multiple_of(where_ref[2] * rows, rows), rows), :]
    total = pull_back(dy, h_ref[...], gain_ref[1:2, :], grad)
    own_ref[...] = total
    for i in range(count):
        spread_ref[i] = total


def settle_back(where, got, dy, h_own, gains):
    count, rows, width = got.shape
    outs = [bf16(rows, width), bf16(count, rows, width)]
    return call(settle_back_kernel, "settle_back", where, [got, dy, h_own, gains], outs)


def half_kernel(where_ref, keep_ref, got_ref, mine_ref, *rest):
    gives, total = rest[:-1], rest[-1]
    total[...] = keep_ref[...].astype(jnp.float32) + got_ref[...].astype(jnp.float32)
    z = where_ref[2] >> 1
    mine_ref[...] = total[z]
    for step, give_ref in enumerate(gives):
        give_ref[...] = total[z ^ (step + 1)].astype(jnp.bfloat16)


def half_sums(where, keep, got):
    groups, rows, width = keep.shape
    return pl.pallas_call(
        half_kernel,
        in_specs=[IN_SMEM] + [IN_VMEM] * 2,
        out_specs=[IN_VMEM] * groups,
        out_shape=[f32(rows, width)] + [bf16(rows, width)] * (groups - 1),
        scratch_shapes=[pltpu.VMEM(keep.shape, jnp.float32)],
        compiler_params=PARAMS,
        cost_estimate=FREE,
        name="half_sums",
    )(where, keep, got)


def last_kernel(x_ref, mine_ref, *rest):
    total = x_ref[...].astype(jnp.float32) + mine_ref[...]
    for got_ref in rest[:-1]:
        total += got_ref[...].astype(jnp.float32)
    rest[-1][...] = total.astype(jnp.bfloat16)


def last_sums(x_own, mine, got):
    return call(last_kernel, "last_sums", None, [x_own, mine, *got], [bf16(*x_own.shape)])[0]


def last_back_kernel(dy_ref, h_ref, gain_ref, mine_ref, *rest):
    grad = mine_ref[...]
    for got_ref in rest[:-1]:
        grad += got_ref[...].astype(jnp.float32)
    rest[-1][...] = pull_back(dy_ref[...], h_ref[...], gain_ref[1:2, :], grad)


def last_back(dy_own, h_own, gains, mine, got):
    return call(last_back_kernel, "last_back", None, [dy_own, h_own, gains, mine, *got], [bf16(*h_own.shape)])[0]


def low_kernel(steps, where_ref, x_ref, gain_ref, wi_ref, wo_ref, n_ref, u_ref, slope_ref, *rest):
    if steps:
        own_ref, keep_ref, give_ref, wi, wo, part_ref, sems = rest
        own_ref[...] = x_ref[pl.ds(pl.multiple_of(where_ref[2] * SLOTS, SLOTS), SLOTS), :]
    else:
        part_ref, wi, wo, sems = rest
    into = bring(wi_ref, 0, wi, sems, 0, 1)
    n_ref[...] = norm_value(x_ref[...].astype(jnp.float32), gain_ref[0:1, :]).astype(jnp.bfloat16)
    for i, (cut, copy) in enumerate(into):
        copy.wait()
        if i == 0:
            out_of = bring(wo_ref, 0, wo, sems, len(into), 1)
        a = jnp.dot(n_ref[...], wi[:, cut], preferred_element_type=jnp.float32)
        u, slope = gelu_both(a)
        u_ref[:, cut] = u.astype(jnp.bfloat16)
        slope_ref[:, cut] = slope
    for cut, copy in out_of:
        copy.wait()
        part = jnp.dot(u_ref[...], wo[:, cut], preferred_element_type=jnp.float32)
        part_ref[:, cut] = part.astype(jnp.bfloat16)
    if steps:
        split_rows(part_ref, where_ref[2], keep_ref, give_ref)


def split_rows(part_ref, shard, keep_ref, give_ref):
    groups = part_ref.shape[0] // (2 * SLOTS)
    for y in range(2):

        @pl.when((shard & 1) == y)
        def _():
            for z in range(groups):
                start = z * 2 * SLOTS
                keep_ref[z] = part_ref[start + y * SLOTS : start + (y + 1) * SLOTS, :]
                give_ref[z] = part_ref[start + (1 - y) * SLOTS : start + (2 - y) * SLOTS, :]


def place_rows(half_ref, other_ref, shard, out_ref):
    for step in range(half_ref.shape[0] // SLOTS):
        for flip, source in enumerate((half_ref, other_ref)):
            start = pl.multiple_of((shard ^ (2 * step) ^ flip) * SLOTS, SLOTS)
            out_ref[pl.ds(start, SLOTS), :] = source[step * SLOTS : (step + 1) * SLOTS, :]


def low_forward(where, x, gains, w_in, w_out, steps):
    rows, width = x.shape
    hidden = w_in.shape[3]
    outs = [bf16(rows, width), bf16(rows, hidden), f32(rows, hidden)]
    buffers = [(width, hidden), (hidden, width)]
    if steps:
        outs += [bf16(SLOTS, width)] + [bf16(rows // (2 * SLOTS), SLOTS, width)] * 2
        buffers.append((rows, width))
    else:
        outs.append(bf16(rows, width))
    copies = len(cuts(hidden)) + len(cuts(width))
    return stream(functools.partial(low_kernel, steps), "low_forward", where, [x, gains], [w_in, w_out], outs, buffers, copies)


def high_kernel(steps, where_ref, *refs):
    if steps:
        half_ref, other_ref, gain_ref, du_ref, wi_ref, n_ref, u_ref, da_ref, keep_ref, give_ref, wi, h_ref, part_ref, sems = refs
    else:
        h_ref, gain_ref, du_ref, wi_ref, n_ref, u_ref, da_ref, part_ref, wi, sems = refs
    into = bring(wi_ref, 1, wi, sems, 0, 1)
    if steps:
        place_rows(half_ref, other_ref, where_ref[2], h_ref)
    n_ref[...] = norm_value(h_ref[...].astype(jnp.float32), gain_ref[1:2, :]).astype(jnp.bfloat16)
    for cut, copy in into:
        copy.wait()
        a = jnp.dot(n_ref[...], wi[:, cut], preferred_element_type=jnp.float32)
        u, slope = gelu_both(a)
        u_ref[:, cut] = u.astype(jnp.bfloat16)
        da_ref[:, cut] = (slope * du_ref[:, cut]).astype(jnp.bfloat16)
    for cut in cuts(wi.shape[0]):
        part = lax.dot_general(da_ref[...], wi[cut, :], NT, preferred_element_type=jnp.float32)
        part_ref[:, cut] = part.astype(jnp.bfloat16)
    if steps:
        split_rows(part_ref, where_ref[2], keep_ref, give_ref)


def high_both(where, h, gains, w_in, du, steps):
    rows, width = du.shape[0], gains.shape[1]
    hidden = w_in.shape[3]
    outs = [bf16(rows, width), bf16(rows, hidden), bf16(rows, hidden)]
    buffers = [(width, hidden)]
    if steps:
        outs += [bf16(rows // (2 * SLOTS), SLOTS, width)] * 2
        buffers += [(rows, width)] * 2
    else:
        outs.append(bf16(rows, width))
    kernel = functools.partial(high_kernel, steps)
    return stream(kernel, "high_both", where, [*h, gains, du], [w_in], outs, buffers, len(cuts(hidden)))


def places(order, rows, path, shard):
    to = lax.broadcasted_iota(jnp.int32, (rows, rows), 0)
    source = lax.broadcasted_iota(jnp.int32, (rows, rows), 1)
    if order == "dispatch":
        far = ((to >> 2) & 7) ^ shard
        block = ((far & 1) << 2) | (far & 2) | (far >> 2)
        wanted = block * 16 + ((to >> 5) ^ path) * 4 + (to & 3)
    else:
        far = (to >> 4) ^ shard
        block = ((far & 1) << 2) | (far >> 1)
        wanted = block * 16 + (to & 15)
    return (source == wanted).astype(jnp.float32).astype(jnp.bfloat16)


def high_grad_kernel(ordered, where_ref, raw_ref, wo_ref, own_ref, du_ref, dy_ref, wo, sems):
    pieces = bring(wo_ref, 1, wo, sems, 0, 0)
    if ordered:
        dy_ref[...] = raw_ref[...]
    else:
        pick = places("dispatch", raw_ref.shape[0], where_ref[3], where_ref[2])
        dy_ref[...] = jnp.dot(pick, raw_ref[...], preferred_element_type=jnp.float32).astype(jnp.bfloat16)
    own_ref[...] = dy_ref[pl.ds(pl.multiple_of(where_ref[2] * SLOTS, SLOTS), SLOTS), :]
    for cut, copy in pieces:
        copy.wait()
        du_ref[:, cut] = lax.dot_general(dy_ref[...], wo[cut, :], NT, preferred_element_type=jnp.float32)


def high_grad(where, raw, w_out, ordered):
    rows, width = raw.shape
    hidden = w_out.shape[2]
    outs = [bf16(SLOTS, width), f32(rows, hidden), bf16(rows, width)]
    kernel = functools.partial(high_grad_kernel, ordered)
    return stream(kernel, "high_grad", where, [raw], [w_out], outs, [(hidden, width)], len(cuts(hidden)))


def low_grad_kernel(steps, where_ref, *refs):
    if steps:
        half_ref, other_ref, slope_ref, wo_ref, da_ref, wo, dh_ref, sems = refs
    else:
        dh_ref, slope_ref, wo_ref, da_ref, wo, sems = refs
    loads = bring(wo_ref, 0, wo, sems, 0, 0)
    if steps:
        place_rows(half_ref, other_ref, where_ref[2], dh_ref)
    for cut, copy in loads:
        copy.wait()
        du = lax.dot_general(dh_ref[...], wo[cut, :], NT, preferred_element_type=jnp.float32)
        da_ref[:, cut] = (du * slope_ref[:, cut]).astype(jnp.bfloat16)


def low_grad(where, dh, w_out, slope, steps):
    rows, hidden = slope.shape
    width = w_out.shape[3]
    outs = [bf16(rows, hidden)]
    kernel = functools.partial(low_grad_kernel, steps)
    buffers = [(hidden, width)] + ([(rows, width)] if steps else [])
    return stream(kernel, "low_grad", where, [*dh, slope], [w_out], outs, buffers, len(cuts(hidden)))[0]


def pair_kernel(level, jobs, where_ref, *refs):
    count = len(jobs)
    groups, used = [], 0
    for _, _, halves in jobs:
        size = 5 + halves
        groups.append(refs[used : used + size])
        used += size
    outs = refs[-1 - 5 * count : -1 - 4 * count]
    scratch = [refs[-1 - 4 * count :][4 * i : 4 * i + 4] for i in range(count)]
    sems = refs[-1]

    def run(which):
        waits = []
        for i, (factor, order, halves) in enumerate(jobs):
            a_ref, *b_refs = groups[i][0], *groups[i][3:]
            right, both, _, raw = scratch[i]
            rows, base = a_ref.shape[0], 8 * i
            half, mine, theirs = rows // 2, pl.ds(0, rows), pl.ds(rows, rows)
            copies = [
                pltpu.make_async_copy(a_ref, both.at[mine, :], sems.at[base + 2]),
                pltpu.make_async_copy(groups[i][1 + which], both.at[theirs, :], sems.at[base + 3]),
            ]
            targets = [raw.at[pl.ds(place * half, half), :] for place in range(4)] if order else []
            if halves == 1:
                copies.append(pltpu.make_async_copy(b_refs[0], right.at[mine, :], sems.at[base + 4]))
            else:
                copies.append(pltpu.make_async_copy(b_refs[0], targets[0], sems.at[base + 4]))
                copies.append(pltpu.make_async_copy(b_refs[1], targets[1], sems.at[base + 5]))
            if order:
                copies.append(pltpu.make_async_copy(b_refs[-2], targets[2], sems.at[base + 6]))
                copies.append(pltpu.make_async_copy(b_refs[-1], targets[3], sems.at[base + 7]))
            else:
                copies.append(pltpu.make_async_copy(b_refs[1 + which], right.at[theirs, :], sems.at[base + 6]))
            for copy in copies:
                copy.start()
            waits.append(copies)
        last = []
        for i, (factor, order, halves) in enumerate(jobs):
            right, both, slots, raw = scratch[i]
            rows = groups[i][0].shape[0]
            for copy in waits[i]:
                copy.wait()
            if order:
                for part in (0, 1) if halves == 2 else (1,):
                    path = where_ref[3] ^ where_ref[level] if part else where_ref[3]
                    pick, span = places(order, rows, path, where_ref[2]), pl.ds(part * rows, rows)
                    value = jnp.dot(pick, raw[span, :], preferred_element_type=jnp.float32)
                    right[span, :] = value.astype(jnp.bfloat16)
            copies = []
            for step, cut in enumerate(cuts(both.shape[1], 2 * BLOCK)):
                slot = step % 2
                if step >= 2:
                    copies[step - 2].wait()
                value = lax.dot_general(both[:, cut], right[...], TN, preferred_element_type=jnp.float32)
                slots[slot] = (value * factor).astype(jnp.bfloat16)
                target = outs[i].at[0, level, cut, :]
                copies.append(pltpu.make_async_copy(slots.at[slot], target, sems.at[8 * i + slot]))
                copies[-1].start()
            last += copies[-2:]
        for copy in last:
            copy.wait()

    @pl.when(where_ref[level] == 1)
    def _():
        run(0)

    @pl.when(where_ref[level] != 1)
    def _():
        run(1)


def pair_grads(where, level, *jobs):
    operands, befores, outs, scratch, settings = [where], [], [], [], []
    for a, a_mate, b, b_mate, before, order in jobs:
        (rows, left), right = a.shape, b[0].shape[1]
        operands += [a, *a_mate, *b, *b_mate]
        befores += [] if before is None else [before]
        outs.append(bf16(1, 2, left, right))
        scratch += [
            pltpu.VMEM((2 * rows, right), jnp.bfloat16),
            pltpu.VMEM((2 * rows, left), jnp.bfloat16),
            pltpu.VMEM((2, min(2 * BLOCK, left), right), jnp.bfloat16),
            pltpu.VMEM((2 * rows if order else SLOTS, right), jnp.bfloat16),
        ]
        settings.append((-0.5 / rows**0.5, order, len(b)))
    return pl.pallas_call(
        functools.partial(pair_kernel, level, settings),
        in_specs=[IN_SMEM] + [ANYWHERE] * (len(operands) + len(befores) - 1),
        out_specs=[ANYWHERE] * len(outs),
        out_shape=outs,
        scratch_shapes=[*scratch, pltpu.SemaphoreType.DMA((8 * len(jobs),))],
        input_output_aliases={len(operands) + i: i for i in range(len(befores))},
        compiler_params=SMALL,
        cost_estimate=FREE,
        name="pair_grads",
    )(*operands, *befores)


def dispatch(spread):
    got = lax.all_to_all(spread, ("path", "shard"), split_axis=0, concat_axis=0, tiled=True)
    return got.reshape(got.shape[0] * got.shape[1], got.shape[2])


def gather_shard(spread):
    got = lax.all_to_all(spread, "shard", split_axis=0, concat_axis=0, tiled=True)
    return got.reshape(got.shape[0] * got.shape[1], got.shape[2])


def scatter_shard(part):
    shards = lax.axis_size("shard")
    blocks = part.reshape(shards, part.shape[0] // shards, part.shape[1])
    return lax.all_to_all(blocks, "shard", split_axis=0, concat_axis=0, tiled=True)


def swap(value, axis, bit):
    return lax.ppermute(value, axis, [(i, i ^ bit) for i in range(lax.axis_size(axis))])


def join(*values):
    return lax.optimization_barrier(jnp.concatenate(values, axis=0))


def gather_steps(own, *others):
    pieces = [swap(own, "shard", bit) for bit in (2, 4, 6)]
    own, *rest = tie(own, *pieces, *others)
    half = join(own, *rest[:3])
    return [half, swap(half, "shard", 1)], rest[3:]


def from_mate(values, *mates):
    paths = lax.axis_size("path")
    mates = mates if len(mates) == len(values) else mates * len(values)
    if paths == 4:
        nears = [swap(v, "path", 1) for v in values]
        sent = [jnp.where(mate == 3, near, v) for near, v, mate in zip(nears, values, mates)]
        return [[near, v] for near, v in zip(nears, sent)]
    me = lax.axis_index("path")
    pairs = []
    for value, mate in zip(values, mates):
        behind = (me - (me ^ mate)) % paths
        mine = value
        for shift in range(1, paths):
            got = lax.ppermute(value, "path", [(i, (i + shift) % paths) for i in range(paths)])
            value, mine = tie(value, jnp.where(behind == shift, got, mine))
        pairs.append([mine, mine])
    return pairs


def along_x(pair):
    if lax.axis_size("path") == 4:
        pair[1] = swap(pair[1], "path", 2)


def body(tokens, routes, cotangent, gains, w_in, w_out, partners):
    paths = lax.axis_size("path")
    shards = lax.axis_size("shard")
    cubes = paths == 4 and shards == 8
    me = lax.axis_index("path")
    shard = lax.axis_index("shard")
    mate_low = partners[0, me] ^ me
    mate_high = partners[1, me] ^ me
    where = jnp.stack([mate_low, mate_high, shard, me])
    none = jnp.int32(0)
    gain = gains[0]
    routes = routes.reshape(-1)

    width, hidden = w_in.shape[2:]

    spread = pack(none, routes, tokens, paths, shards)
    x = dispatch(spread)
    if cubes:
        by_path = pack(me, routes, cotangent, paths, 0)
        rows_1 = join(by_path[0], *[swap(by_path[k], "path", k) for k in (1, 2, 3)])
        hop_1 = swap(rows_1, "shard", 4)
        x, hop_1, where, mate_low, mate_high = tie(x, hop_1, where, mate_low, mate_high)
    n1, u1, slope1, *parts = low_forward(where, x, gain, w_in, w_out, cubes)

    (n1_mate,) = from_mate([n1], mate_low)
    if cubes:
        x_own, keep, give = parts
        rows_2 = join(rows_1, hop_1)
        got, hop_2, n1_mate[1] = tie(swap(give, "shard", 1), swap(rows_2, "shard", 2), n1_mate[1])
        along_x(n1_mate)
        mine, *gives = half_sums(where, keep, got)
        got = [swap(gives[k], "shard", 2 * k + 2) for k in (1, 0, 2)]
        rows_4 = join(tie(rows_2, mine)[0], hop_2)
        *got, hop_3 = tie(*got, swap(rows_4, "shard", 1))
        h_own = last_sums(x_own, mine, got)
    else:
        along_x(n1_mate)
        h_own, h_spread = settle(where, scatter_shard(parts[0]), x)

    (u1_mate,) = from_mate([u1], mate_low)
    if cubes:
        (half_mate,) = from_mate([rows_4], mate_high)
        dy_own, du2, dy = high_grad(where, join(rows_4, hop_3), w_out, False)
        h, (n1_mate[1], u1_mate[1], half_mate[1]) = gather_steps(h_own, n1_mate[1], u1_mate[1], half_mate[1])
        along_x(u1_mate)
        along_x(half_mate)
        *h, u1_mate[1], du2 = tie(*h, u1_mate[1], du2)
    else:
        h = [gather_shard(h_spread)]
        along_x(u1_mate)
        dy = dispatch(pack(none, routes, cotangent, paths, shards))
        dy_own, du2, dy = high_grad(where, dy, w_out, True)
    n2, u2, da2, *parts = high_both(where, h, gain, w_in, du2, cubes)

    da2_mate, u2_mate = from_mate([da2, u2], mate_high)
    if cubes:
        keep, give = parts
        got, da2_mate[1], half_mate[1] = tie(swap(give, "shard", 1), da2_mate[1], half_mate[1])
        along_x(da2_mate)
        mine, *gives = half_sums(where, keep, got)
        got = [swap(gives[k], "shard", 2 * k + 2) for k in (1, 0, 2)]
        half = jnp.where(mate_high == 1, *half_mate)
        hop_4 = swap(tie(half, mine)[0], "shard", 1)
        *got, hop_4, da2_mate[1], u2_mate[1] = tie(*got, hop_4, da2_mate[1], u2_mate[1])
        along_x(u2_mate)
        dh_own = last_back(dy_own, h_own, gain, mine, got)
    else:
        along_x(da2_mate)
        along_x(u2_mate)
        dh_own, dh_spread = settle_back(where, scatter_shard(parts[0]), dy, h_own, gain)

    (n2_mate,) = from_mate([n2], mate_high)
    if cubes:
        (dh_pair,) = from_mate([dh_own], mate_low)
        dh_own, dh_pair[1] = tie(dh_own, dh_pair[1])
        along_x(dh_pair)
        dh_piece = jnp.where(mate_low == 1, *dh_pair)
        dh, (u2_mate[1], n2_mate[1], dh_piece) = gather_steps(dh_own, u2_mate[1], n2_mate[1], dh_piece)
        along_x(n2_mate)
        pieces = [swap(dh_piece, "shard", bit) for bit in (2, 4, 6)]
        dy_mate = [half, hop_4]
    else:
        along_x(n2_mate)
        dh = [gather_shard(dh_spread)]
    da1 = low_grad(where, dh, w_out, slope1, cubes)

    if cubes:
        da1, n2_mate[1], *pieces = tie(da1, n2_mate[1], *pieces)
    (da1_mate,) = from_mate([da1], mate_low)
    along_x(da1_mate)
    if cubes:
        dh_half = join(dh_piece, *pieces)
        dh_mate = [dh_half, swap(dh_half, "shard", 1)]
    else:
        (dh_mate,) = from_mate(dh, mate_low)
        along_x(dh_mate)
        (dy_mate,) = from_mate([dy], mate_high)
        along_x(dy_mate)
    delta_in, delta_out = pair_grads(
        where,
        1,
        (n2, n2_mate, [da2], da2_mate, None, ""),
        (u2, u2_mate, [dy], dy_mate, None, "dispatch" if cubes else ""),
    )
    delta_in, delta_out = pair_grads(
        where,
        0,
        (n1, n1_mate, [da1], da1_mate, delta_in, ""),
        (u1, u1_mate, dh, dh_mate, delta_out, "gather" if cubes else ""),
    )
    return (delta_in, delta_out)


def solution(mesh):
    in_specs = (
        P(("path", "shard"), None),
        P(("path", "shard"), None),
        P(("path", "shard"), None),
        P("path", None, None),
        P("path", None, None, "shard"),
        P("path", None, "shard", None),
        P(),
    )
    out_specs = (P("path", None, None, "shard"), P("path", None, "shard", None))
    return jax.shard_map(body, mesh=mesh, in_specs=in_specs, out_specs=out_specs, check_vma=False)
```
